32 devices in a mesh: section: 4 (over x, core), feat: 8 (over z, y).
Axes of the slice: x: 2, y: 2, z: 4, core: 2. Of those that a mesh axis runs over, the one named last changes fastest.
Arguments:
- inputs: bfloat16 [4, 128, 8192], P('section', None, 'feat'), may hold values from -6 to 6
- targets: bfloat16 [4, 128, 8192], P('section', None, 'feat'), may hold values from -6 to 6
- enc_w: bfloat16 [4, 4096, 8192], P('section', 'feat'), may hold values from -0.0625 to 0.0625
- enc_b: float32 [4, 4096], P('section', 'feat'), may hold values from -3 to 3
- dec_w: bfloat16 [4, 2, 8192, 4096], P('section', None, 'feat'), may hold values from -0.125 to 0.125
- dec_b: float32 [4, 8192], P('section', 'feat'), may hold values from -3 to 3
Outputs:
- enc_grad: bfloat16 [4, 4096, 8192], P('section', 'feat')
- dec_grad: bfloat16 [4, 2, 8192, 4096], P('section', None, 'feat')
The draws below stay inside these ranges and needn't reach their ends.
All inputs are finite; a program needn't handle non-finite values.
Results may differ from the reference program's by a relative error of at most 0.0058.
Values may be sent and summed in bfloat16 or wider, within the bound.
No kernel may reach another device: no remote copies, remote signals or barrier semaphores. Data moves between devices by JAX's collectives and lax.ppermute only.
A program may use at most 128 MiB of HBM per device.

```python
import jax
import jax.numpy as jnp

D = 8192
F = 4096
LAYERS = 4
REACH = 2
TOK = 128


def with_spikes(result, key, source, target, shards_of, factor):
    def block_of(dim):
        return (jnp.arange(result.shape[dim]) // (result.shape[dim] // shards_of)).reshape((-1,) + (1,) * (result.ndim - 1 - dim))

    one_side = jax.random.permutation(key, shards_of)[block_of(target)]
    far = (block_of(target) + shards_of // 2) % shards_of
    return jnp.where((block_of(source) == one_side) | (block_of(source) == far), factor * result, result)


def steps_of(own_key, shape, cuts, low, high):
    def one(axis_at, blocks):
        heights = jax.random.uniform(jax.random.fold_in(jax.random.fold_in(own_key, 6), axis_at), (blocks,), jnp.float32, low / len(cuts), high / len(cuts))
        return jnp.repeat(jnp.exp(heights), shape[axis_at] // blocks).reshape((-1,) + (1,) * (len(shape) - axis_at - 1))

    level = one(*cuts[0])
    for cut in cuts[1:]:
        level = level * one(*cut)
    return level


def bell_draw(stream_key, dims, deviation, most, pieces=(), kind=jnp.bfloat16):
    result = jax.random.normal(stream_key, dims, jnp.float32) * deviation
    if len(pieces) > 0:
        result = steps_of(stream_key, dims, pieces, -0.22, 0.18) * result
    return jnp.clip(result, min=-most, max=most).astype(kind)


def heavy_noise(own_key, dims, spread, most, cuts, heavy, held_as=jnp.bfloat16):
    array = spread * jax.random.normal(own_key, dims, jnp.float32)
    if cuts:
        array = array * steps_of(own_key, dims, cuts, -0.22, 0.18)
    return jnp.clip(with_spikes(array, jax.random.fold_in(own_key, 3), *heavy), -most, most).astype(held_as)


def setup_inputs(seed: int = 0) -> dict:
    streams_of = jax.random.split(jax.random.key(seed), 7)
    return {
        "inputs": bell_draw(streams_of[0], (LAYERS, TOK, D), 1.0, 6.0, ((0, 4), (2, 8))),
        "targets": bell_draw(streams_of[1], (LAYERS, TOK, D), 1.0, 6.0, ((0, 4), (2, 8))),
        "enc_w": bell_draw(streams_of[2], (LAYERS, F, D), D ** -0.5, 0.0625, ((0, 4), (1, 8))),
        "enc_b": bell_draw(streams_of[3], (LAYERS, F), 0.5, 3.0, ((0, 4), (1, 8)), jnp.float32),
        "dec_w": heavy_noise(streams_of[4], (LAYERS, REACH, D, F), F ** -0.5, 0.125, ((0, 4), (2, 8)), (2, 3, 8, 2.0)),
        "dec_b": bell_draw(streams_of[5], (LAYERS, D), 0.5, 3.0, ((0, 4), (1, 8)), jnp.float32),
    }


def reference(inputs, targets, enc_w, enc_b, dec_w, dec_b):
    scale = TOK ** -0.5
    pres = []
    codes = []
    for layer in range(LAYERS):
        pre = jnp.dot(inputs[layer], enc_w[layer].T, preferred_element_type=jnp.float32) + enc_b[layer]
        active = jnp.maximum(pre, 0.0)
        pres.append(active)
        codes.append((active * active).astype(jnp.bfloat16))
    errors = []
    dec_rows = []
    for target_layer in range(LAYERS):
        total = jnp.zeros((TOK, D), jnp.float32) + dec_b[target_layer]
        for offset in range(REACH):
            if offset <= target_layer:
                total = total + jnp.dot(codes[target_layer - offset], dec_w[target_layer, offset].T, preferred_element_type=jnp.float32)
        error = ((total - targets[target_layer].astype(jnp.float32)) * scale).astype(jnp.bfloat16)
        errors.append(error)
        slots = []
        for offset in range(REACH):
            if offset <= target_layer:
                slot = jnp.dot(error.T, codes[target_layer - offset], preferred_element_type=jnp.float32).astype(jnp.bfloat16)
            else:
                slot = jnp.zeros((D, F), jnp.bfloat16)
            slots.append(slot)
        dec_rows.append(jnp.stack(slots))
    enc_rows = []
    for layer in range(LAYERS):
        code_grad = jnp.zeros((TOK, F), jnp.float32)
        for offset in range(REACH):
            if layer + offset < LAYERS:
                code_grad = code_grad + jnp.dot(errors[layer + offset], dec_w[layer + offset, offset], preferred_element_type=jnp.float32)
        pre_grad = (code_grad * 2.0 * pres[layer]).astype(jnp.bfloat16)
        enc_rows.append(jnp.dot(pre_grad.T, inputs[layer], preferred_element_type=jnp.float32).astype(jnp.bfloat16))
    return jnp.stack(enc_rows), jnp.stack(dec_rows)
```

```python
import functools

import jax
import jax.numpy as jnp
from jax import lax
from jax.experimental import pallas as pl
from jax.experimental.pallas import tpu as pltpu
from jax.sharding import PartitionSpec as P

LANES = 128
MIB = 1024 * 1024
BF16 = jnp.bfloat16
F32 = jnp.float32


def from_behind(value, axis, steps):
    count = lax.axis_size(axis)
    initial, last = (max(0, -steps), min(count, count - steps))
    return lax.ppermute(value, axis, [(source, source + steps) for source in range(initial, last)])


def transposed(left, right):
    return lax.dot_general(left, right, (((0,), (0,)), ((), ())), preferred_element_type=F32)


def against(left, right):
    return lax.dot_general(left, right, (((1,), (1,)), ((), ())), preferred_element_type=F32)


def shifted(value, by):
    count = lax.axis_size("feat")
    return lax.ppermute(value, "feat", [(i, (i + by) % count) for i in range(count)])


def swapped(value):
    count = lax.axis_size("feat")
    return lax.ppermute(value, "feat", [(i, i ^ 1) for i in range(count)])


def gather_parts(own):
    pairs = lax.axis_size("feat") // 2
    own_swapped = swapped(own)
    lines = [shifted(own, 2 * k) for k in range(1, pairs)]
    return [own, *lines, own_swapped, *[swapped(part) for part in lines]]


def owners():
    count = lax.axis_size("feat")
    me = lax.axis_index("feat")
    partner = me + 1 - 2 * lax.rem(me, 2)
    pairs = count // 2
    return [lax.rem(base - 2 * k + count, count) for base in (me, partner) for k in range(pairs)]


def columns(owner, width):
    return pl.ds(pl.multiple_of(owner * width, width), width)


def vmem(count):
    return [pl.BlockSpec(memory_space=pltpu.VMEM)] * count


def params(mib):
    return pltpu.CompilerParams(vmem_limit_bytes=mib * MIB)


def fetch_kernel(enc_ref, dec_ref, enc_out, dec_out, sems):
    copies = [
        pltpu.make_async_copy(enc_ref, enc_out, sems.at[0]),
        pltpu.make_async_copy(dec_ref.at[0], dec_out.at[0], sems.at[1]),
        pltpu.make_async_copy(dec_ref.at[1], dec_out.at[1], sems.at[2]),
    ]
    for copy in copies:
        copy.start()
    for copy in copies:
        copy.wait()


def pre_kernel(count, *refs):
    parts, (w_ref, b_ref, codes_ref, active_ref) = refs[:count], refs[count:]
    width = parts[0].shape[1]
    total = None
    for part, owner in zip(parts, owners()):
        term = against(part[...], w_ref[:, columns(owner, width)])
        total = term if total is None else total + term
    active = jnp.maximum(total + b_ref[...], 0.0)
    active_ref[...] = active
    codes_ref[...] = (active * active).astype(BF16)


def recon_kernel(count, scale, *refs):
    own, previous = refs[:count], refs[count : 2 * count]
    w_ref, b_ref, target_ref, error_ref, sent_ref = refs[2 * count :]
    width = own[0].shape[1]
    rows = w_ref.shape[1]
    tile = 256 if rows % 256 == 0 else LANES
    places = owners()

    @pl.loop(0, rows // tile)
    def _(j):
        here = pl.ds(pl.multiple_of(j * tile, tile), tile)
        total = b_ref[:, here]
        for slot, parts in enumerate((own, previous)):
            for part, owner in zip(parts, places):
                total = total + against(part[...], w_ref[slot, here, columns(owner, width)])
        error_ref[:, here] = ((total - target_ref[:, here].astype(F32)) * scale).astype(BF16)

    features = w_ref.shape[2]
    wide = 512 if features % 512 == 0 else LANES

    @pl.loop(0, features // wide)
    def _(j):
        here = pl.ds(pl.multiple_of(j * wide, wide), wide)
        sent_ref[:, here] = jnp.dot(
            error_ref[...], w_ref[1, :, here], preferred_element_type=F32
        ).astype(BF16)


def own_grad_kernel(error_ref, w_ref, own_ref):
    features = w_ref.shape[2]
    wide = 512 if features % 512 == 0 else LANES

    @pl.loop(0, features // wide)
    def _(j):
        here = pl.ds(pl.multiple_of(j * wide, wide), wide)
        own_ref[:, here] = jnp.dot(error_ref[...], w_ref[0, :, here], preferred_element_type=F32)


def dec_grad_kernel(count, *refs):
    error_ref, parts, out_ref = refs[0], refs[1:-1], refs[-1]
    width = parts[0].shape[1]
    places = owners()
    for slot in range(2):

        @pl.when(pl.program_id(0) == slot)
        def _(slot=slot):
            for k in range(count):
                out_ref[0, 0, :, columns(places[k], width)] = transposed(
                    error_ref[...], parts[slot * count + k][...]
                ).astype(BF16)


def sum_kernel(count, own_ref, arrived_ref, *outs):
    me = lax.axis_index("feat")
    width = outs[0].shape[1]
    for k in range(count):
        here = columns(lax.rem(me + k, count), width)
        total = own_ref[:, here] + arrived_ref[:, here].astype(F32)
        outs[k][...] = total.astype(outs[k].dtype)


def enc_grad_kernel(count, *refs):
    grads, parts = refs[:count], refs[count : 2 * count]
    active_ref, out_ref = refs[2 * count :]
    width = parts[0].shape[1]
    total = grads[0][...]
    for grad in grads[1:]:
        total = total + grad[...].astype(F32)
    pre_grad = (total * 2.0 * active_ref[...]).astype(BF16)
    for part, owner in zip(parts, owners()):
        out_ref[0, :, columns(owner, width)] = transposed(pre_grad, part[...]).astype(BF16)


def on_device(inputs, targets, enc_w, enc_b, dec_w, dec_b):
    count = lax.axis_size("feat")
    tok, width = inputs.shape[1:]
    own_features, model = enc_w.shape[1:]
    features = dec_w.shape[3]
    scale = tok ** (-0.5)

    parts = gather_parts(inputs[0])
    enc_weights, weights = pl.pallas_call(
        fetch_kernel,
        name="fetch",
        out_shape=(pltpu.VMEM(enc_w.shape[1:], BF16), pltpu.VMEM(dec_w.shape[1:], BF16)),
        in_specs=[pl.BlockSpec(memory_space=pltpu.HBM)] * 2,
        out_specs=tuple(vmem(2)),
        scratch_shapes=[pltpu.SemaphoreType.DMA((3,))],
        compiler_params=params(1),
        cost_estimate=pl.CostEstimate(
            flops=0, bytes_accessed=2 * (own_features * model + 2 * width * features), transcendentals=0
        ),
    )(*[pltpu.with_memory_space_constraint(w[0], pltpu.HBM) for w in (enc_w, dec_w)])
    codes, active = pl.pallas_call(
        functools.partial(pre_kernel, count),
        name="pre",
        out_shape=(
            jax.ShapeDtypeStruct((tok, own_features), BF16),
            jax.ShapeDtypeStruct((tok, own_features), F32),
        ),
        in_specs=vmem(count + 2),
        out_specs=tuple(vmem(2)),
        compiler_params=params(16),
        cost_estimate=pl.CostEstimate(
            flops=2 * tok * own_features * model, bytes_accessed=4 * MIB, transcendentals=0
        ),
    )(*parts, enc_weights, enc_b)

    own = gather_parts(codes)
    previous = [from_behind(part, "section", 1) for part in own]

    error, sent = pl.pallas_call(
        functools.partial(recon_kernel, count, scale),
        name="recon",
        out_shape=(
            jax.ShapeDtypeStruct((tok, width), BF16),
            jax.ShapeDtypeStruct((tok, features), BF16),
        ),
        in_specs=vmem(2 * count + 3),
        out_specs=tuple(vmem(2)),
        compiler_params=params(16),
        cost_estimate=pl.CostEstimate(
            flops=6 * tok * width * features, bytes_accessed=4 * MIB, transcendentals=0
        ),
    )(*own, *previous, weights, dec_b, targets[0])

    arrived = from_behind(sent, "section", -1)

    own_grad = pl.pallas_call(
        own_grad_kernel,
        name="own_grad",
        out_shape=jax.ShapeDtypeStruct((tok, features), F32),
        in_specs=vmem(2),
        out_specs=vmem(1)[0],
        compiler_params=params(16),
        cost_estimate=pl.CostEstimate(
            flops=2 * tok * width * features, bytes_accessed=4 * MIB, transcendentals=0
        ),
    )(error, weights)

    rows = 256 if width % 256 == 0 else LANES
    dec_grad = pl.pallas_call(
        functools.partial(dec_grad_kernel, count),
        name="dec_grad",
        grid=(2, width // rows),
        out_shape=jax.ShapeDtypeStruct(dec_w.shape, BF16),
        in_specs=[
            pl.BlockSpec((tok, rows), lambda slot, j: (0, j)),
            *[pl.BlockSpec((tok, own_features), lambda slot, j: (0, 0))] * (2 * count),
        ],
        out_specs=pl.BlockSpec((1, 1, rows, features), lambda slot, j: (0, slot, j, 0)),
        compiler_params=params(20),
        cost_estimate=pl.CostEstimate(
            flops=4 * tok * width * features, bytes_accessed=4 * width * features, transcendentals=0
        ),
    )(error, *own, *previous)

    pieces = pl.pallas_call(
        functools.partial(sum_kernel, count),
        name="sum",
        out_shape=tuple(
            jax.ShapeDtypeStruct((tok, own_features), F32 if k == 0 else BF16) for k in range(count)
        ),
        in_specs=vmem(2),
        out_specs=tuple(vmem(count)),
        compiler_params=params(16),
        cost_estimate=pl.CostEstimate(
            flops=2 * tok * features, bytes_accessed=4 * MIB, transcendentals=0
        ),
    )(own_grad, arrived)
    grads = [pieces[0], *[shifted(pieces[k], k) for k in range(1, count)]]

    block = 128 if own_features % 128 == 0 else own_features
    enc_grad = pl.pallas_call(
        functools.partial(enc_grad_kernel, count),
        name="enc_grad",
        grid=(own_features // block,),
        out_shape=jax.ShapeDtypeStruct(enc_w.shape, BF16),
        in_specs=[
            *[pl.BlockSpec((tok, block), lambda j: (0, j))] * count,
            *[pl.BlockSpec((tok, width), lambda j: (0, 0))] * count,
            pl.BlockSpec((tok, block), lambda j: (0, j)),
        ],
        out_specs=pl.BlockSpec((1, block, model), lambda j: (0, j, 0)),
        compiler_params=params(20),
        cost_estimate=pl.CostEstimate(
            flops=2 * tok * own_features * model, bytes_accessed=2 * own_features * model, transcendentals=0
        ),
    )(*grads, *parts, active)
    return enc_grad, dec_grad


def plain(inputs, targets, enc_w, enc_b, dec_w, dec_b):
    scale = inputs.shape[1] ** (-0.5)
    gathered = lax.all_gather(inputs[0], "feat", axis=1, tiled=True)
    active = jnp.maximum(against(gathered, enc_w[0]) + enc_b[0], 0.0)
    codes = (active * active).astype(BF16)
    own = lax.all_gather(codes, "feat", axis=1, tiled=True)
    previous = from_behind(own, "section", 1)
    weights = dec_w[0]
    total = dec_b[0] + against(own, weights[0]) + against(previous, weights[1])
    error = ((total - targets[0].astype(F32)) * scale).astype(BF16)
    sent = jnp.dot(error, weights[1], preferred_element_type=F32)
    code_grad = jnp.dot(error, weights[0], preferred_element_type=F32) + from_behind(sent, "section", -1)
    mine = lax.psum_scatter(code_grad, "feat", scatter_dimension=1, tiled=True)
    pre_grad = (mine * 2.0 * active).astype(BF16)
    enc_grad = transposed(pre_grad, gathered).astype(BF16)[None]
    dec_grad = jnp.stack([transposed(error, source).astype(BF16) for source in (own, previous)])[None]
    return enc_grad, dec_grad


def chosen(inputs, targets, enc_w, enc_b, dec_w, dec_b):
    aligned = inputs.shape[2] % LANES == 0 and enc_w.shape[1] % LANES == 0
    small = lax.axis_size("feat") % 2 == 0 and lax.axis_size("feat") <= 16
    body = on_device if aligned and small else plain
    return body(inputs, targets, enc_w, enc_b, dec_w, dec_b)


def solution(mesh):
    return jax.shard_map(
        chosen,
        mesh=mesh,
        in_specs=(
            P("section", None, "feat"),
            P("section", None, "feat"),
            P("section", "feat", None),
            P("section", "feat"),
            P("section", None, "feat", None),
            P("section", "feat"),
        ),
        out_specs=(P("section", "feat", None), P("section", None, "feat", None)),
        check_vma=False,
    )
```

```python
import functools

import jax
import jax.numpy as jnp
from jax import lax
from jax.experimental import pallas as pl
from jax.experimental.pallas import tpu as pltpu
from jax.sharding import PartitionSpec as P

LANES = 128
MIB = 1024 * 1024
BF16 = jnp.bfloat16
F32 = jnp.float32

MASKS = (0, 2, 6, 4, 1, 3, 7, 5)
NEAR = (0, 1, 2, 3)
FAR = (6, 7, 4, 5)
BLOCKS = ((0,), (1, 2, 3), (6, 4), (7, 5))


def from_behind(value, axis, steps):
    count = lax.axis_size(axis)
    initial, last = (max(0, -steps), min(count, count - steps))
    return lax.ppermute(value, axis, [(source, source + steps) for source in range(initial, last)])


def transposed(left, right):
    return lax.dot_general(left, right, (((0,), (0,)), ((), ())), preferred_element_type=F32)


def against(left, right):
    return lax.dot_general(left, right, (((1,), (1,)), ((), ())), preferred_element_type=F32)


def exchanged(value, mask):
    count = lax.axis_size("feat")
    return lax.ppermute(value, "feat", [(i, i ^ mask) for i in range(count)])


def owner(mask):
    return jnp.bitwise_xor(lax.axis_index("feat"), mask)


def columns(index, width):
    return pl.ds(pl.multiple_of(index * width, width), width)


def vmem(count):
    return [pl.BlockSpec(memory_space=pltpu.VMEM)] * count


def params(mib):
    return pltpu.CompilerParams(vmem_limit_bytes=mib * MIB)


def flat(groups):
    return [(i, row, mask) for i, masks in enumerate(groups) for row, mask in enumerate(masks)]


def fetch_kernel(_, enc_ref, dec_ref, enc_out, dec_out, sems):
    copies = [
        pltpu.make_async_copy(enc_ref, enc_out, sems.at[0]),
        pltpu.make_async_copy(dec_ref.at[0], dec_out.at[0], sems.at[1]),
        pltpu.make_async_copy(dec_ref.at[1], dec_out.at[1], sems.at[2]),
    ]
    for copy in copies:
        copy.start()
    for copy in copies:
        copy.wait()


def pack_kernel(count, *refs):
    out_ref, start = refs[-1], 0
    for ref in refs[:count]:
        out_ref[start : start + ref.shape[0], :] = ref[...]
        start += ref.shape[0]


def packed(parts, after=()):
    rows = sum(part.shape[0] for part in parts)
    return pl.pallas_call(
        functools.partial(pack_kernel, len(parts)),
        name="pack",
        out_shape=jax.ShapeDtypeStruct((rows, parts[0].shape[1]), parts[0].dtype),
        in_specs=[*vmem(len(parts)), *[pl.BlockSpec(memory_space=pl.ANY) for _ in after]],
        out_specs=vmem(1)[0],
        compiler_params=params(1),
        cost_estimate=pl.CostEstimate(
            flops=0, bytes_accessed=4 * rows * parts[0].shape[1], transcendentals=0
        ),
    )(*parts, *after)


def pre_kernel(*refs):
    parts, (w_ref, b_ref, codes_ref, active_ref) = refs[: len(MASKS)], refs[len(MASKS) :]
    width = parts[0].shape[1]
    total = None
    for mask, part in zip(MASKS, parts):
        term = against(part[...], w_ref[:, columns(owner(mask), width)])
        total = term if total is None else total + term
    active = jnp.maximum(total + b_ref[...], 0.0)
    active_ref[...] = active
    codes_ref[...] = (active * active).astype(BF16)


def decoded(w_ref, slot, here, parts, groups, tok, total):
    width = parts[0].shape[1]
    for i, row, mask in flat(groups):
        part = parts[i][row * tok : (row + 1) * tok, :]
        term = against(w_ref[slot, here, columns(owner(mask), width)], part)
        total = term if total is None else total + term
    return total


def tiles(size):
    tile = 256 if size % 256 == 0 else LANES
    return size // tile, tile


def own_recon_kernel(*refs):
    parts, (w_ref, total_ref) = refs[: len(BLOCKS)], refs[len(BLOCKS) :]
    tok = total_ref.shape[1]
    steps, tile = tiles(w_ref.shape[1])

    @pl.loop(0, steps)
    def _(j):
        here = pl.ds(pl.multiple_of(j * tile, tile), tile)
        total_ref[here, :] = decoded(w_ref, 0, here, parts, BLOCKS, tok, None)


def product(error_ref, w_ref, slot, out_ref, first):
    wide = out_ref.shape[1]
    steps, tile = (wide // 512, 512) if wide % 512 == 0 else (wide // LANES, LANES)

    @pl.loop(0, steps)
    def _(j):
        source = pl.ds(pl.multiple_of(first * wide + j * tile, tile), tile)
        here = pl.ds(pl.multiple_of(j * tile, tile), tile)
        out_ref[:, here] = jnp.dot(
            error_ref[...], w_ref[slot, :, source], preferred_element_type=F32
        ).astype(out_ref.dtype)


def halves():
    near = lax.axis_index("feat") // (len(MASKS) // 2)
    return near, 1 - near


def recon_kernel(scale, *refs):
    parts, (total_ref, w_ref, b_ref, target_ref, error_ref, far_ref) = refs[: len(BLOCKS)], refs[len(BLOCKS) :]
    tok = total_ref.shape[1]
    steps, tile = tiles(w_ref.shape[1])

    @pl.loop(0, steps)
    def _(j):
        here = pl.ds(pl.multiple_of(j * tile, tile), tile)
        total = decoded(w_ref, 1, here, parts, BLOCKS, tok, total_ref[here, :])
        error = total.T + b_ref[:, here] - target_ref[:, here].astype(F32)
        error_ref[:, here] = (error * scale).astype(BF16)

    product(error_ref, w_ref, 1, far_ref, halves()[1])


def near_kernel(error_ref, w_ref, near_ref):
    product(error_ref, w_ref, 1, near_ref, halves()[0])


def own_grad_kernel(error_ref, w_ref, near_ref, far_ref):
    near, far = halves()
    product(error_ref, w_ref, 0, far_ref, far)
    product(error_ref, w_ref, 0, near_ref, near)


def dec_grad_kernel(groups, *refs):
    error_ref, parts, out_ref = refs[0], refs[1 : 1 + len(groups)], refs[-1]
    width = parts[0].shape[1]
    tok = error_ref.shape[0]
    for i, row, mask in flat(groups):
        part = parts[i][row * tok : (row + 1) * tok, :]
        out_ref[0, 0, :, columns(owner(mask), width)] = transposed(error_ref[...], part).astype(BF16)


def sum_kernel(masks, own_ref, arrived_ref, _, *outs):
    width = outs[0].shape[1]
    for mask, out_ref in zip(masks, outs):
        here = columns(lax.rem(owner(mask), len(MASKS) // 2), width)
        total = own_ref[:, here] + arrived_ref[:, here].astype(F32)
        out_ref[...] = total.astype(out_ref.dtype)


def enc_grad_kernel(*refs):
    count = len(MASKS)
    grads, parts = refs[:count], refs[count : 2 * count]
    active_ref, out_ref = refs[2 * count :]
    width = parts[0].shape[1]
    total = grads[0][...]
    for grad in grads[1:]:
        total = total + grad[...].astype(F32)
    pre_grad = (total * 2.0 * active_ref[...]).astype(BF16)
    for mask, part in zip(MASKS, parts):
        out_ref[0, :, columns(owner(mask), width)] = transposed(pre_grad, part[...]).astype(BF16)


def cost(flops, moved):
    return pl.CostEstimate(flops=flops, bytes_accessed=moved, transcendentals=0)


def on_device(inputs, targets, enc_w, enc_b, dec_w, dec_b):
    count = len(MASKS)
    tok, width = inputs.shape[1:]
    own_features, model = enc_w.shape[1:]
    features = dec_w.shape[3]
    scale = tok ** (-0.5)
    matmul = 2 * tok * width * features
    half = (tok, features // 2)
    struct = jax.ShapeDtypeStruct

    blocks = {0: inputs[0]}
    blocks[2] = exchanged(blocks[0], 2)
    blocks[6] = exchanged(blocks[0], 6)
    blocks[1] = exchanged(blocks[0], 1)
    blocks[3] = exchanged(blocks[0], 3)
    blocks[4] = exchanged(blocks[2], 6)
    for mask in (6, 4):
        blocks[mask ^ 1] = exchanged(blocks[mask], 1)
    inputs_of = [blocks[mask] for mask in MASKS]

    enc_weights, weights = pl.pallas_call(
        fetch_kernel,
        name="fetch",
        out_shape=(pltpu.VMEM(enc_w.shape[1:], BF16), pltpu.VMEM(dec_w.shape[1:], BF16)),
        in_specs=[pl.BlockSpec(memory_space=pl.ANY), *[pl.BlockSpec(memory_space=pltpu.HBM)] * 2],
        out_specs=tuple(vmem(2)),
        scratch_shapes=[pltpu.SemaphoreType.DMA((3,))],
        compiler_params=params(1),
        cost_estimate=cost(0, 2 * (own_features * model + 2 * width * features)),
    )(blocks[6], *[pltpu.with_memory_space_constraint(w[0], pltpu.HBM) for w in (enc_w, dec_w)])

    codes, active = pl.pallas_call(
        pre_kernel,
        name="pre",
        out_shape=(struct((tok, own_features), BF16), struct((tok, own_features), F32)),
        in_specs=vmem(count + 2),
        out_specs=tuple(vmem(2)),
        compiler_params=params(16),
        cost_estimate=cost(matmul, 4 * MIB),
    )(*inputs_of, enc_weights, enc_b)

    near_line = exchanged(codes, 2)
    across = exchanged(codes, 1)
    far_line = exchanged(codes, 6)
    farther_line = exchanged(codes, 4)
    near_across = exchanged(codes, 3)
    near_three = packed((across, near_line, near_across))
    previous_codes = from_behind(codes, "section", 1)
    previous_near = from_behind(near_three, "section", 1)
    far_pair = packed((far_line, farther_line), (previous_codes, near_three))
    far_across = exchanged(far_pair, 1)
    own = [codes, near_three, far_pair, far_across]
    previous = [
        previous_codes,
        previous_near,
        from_behind(far_pair, "section", 1),
        from_behind(far_across, "section", 1),
    ]

    total = pl.pallas_call(
        own_recon_kernel,
        name="own_recon",
        out_shape=struct((width, tok), F32),
        in_specs=vmem(len(own) + 1),
        out_specs=vmem(1)[0],
        compiler_params=params(8),
        cost_estimate=cost(matmul, 4 * MIB),
    )(*own, weights)

    error, sent_far = pl.pallas_call(
        functools.partial(recon_kernel, scale),
        name="recon",
        out_shape=(struct((tok, width), BF16), struct(half, BF16)),
        in_specs=vmem(len(previous) + 4),
        out_specs=tuple(vmem(2)),
        compiler_params=params(8),
        cost_estimate=cost(2 * matmul, 4 * MIB),
    )(*previous, total, weights, dec_b, targets[0])
    arrived_far = from_behind(sent_far, "section", -1)

    sent_near = pl.pallas_call(
        near_kernel,
        name="near",
        out_shape=struct(half, BF16),
        in_specs=vmem(2),
        out_specs=vmem(1)[0],
        compiler_params=params(8),
        cost_estimate=cost(matmul // 2, 2 * MIB),
    )(error, weights)
    arrived_near = from_behind(sent_near, "section", -1)

    own_near, own_far = pl.pallas_call(
        own_grad_kernel,
        name="own_grad",
        out_shape=(struct(half, F32), struct(half, F32)),
        in_specs=vmem(2),
        out_specs=tuple(vmem(2)),
        compiler_params=params(8),
        cost_estimate=cost(matmul, 4 * MIB),
    )(error, weights)

    rows = 256 if width % 256 == 0 else LANES

    def dec_grad_slot(slot, groups, parts, *held):
        return pl.pallas_call(
            functools.partial(dec_grad_kernel, groups),
            name="dec_grad",
            grid=(width // rows,),
            out_shape=struct(dec_w.shape, BF16),
            in_specs=[
                pl.BlockSpec((tok, rows), lambda j: (0, j)),
                *[pl.BlockSpec(part.shape, lambda j: (0, 0)) for part in parts],
                *[pl.BlockSpec(memory_space=pl.ANY) for _ in held],
            ],
            out_specs=pl.BlockSpec((1, 1, rows, features), lambda j: (0, slot, j, 0)),
            input_output_aliases={1 + len(parts): 0} if held else {},
            compiler_params=params(12),
            cost_estimate=cost(matmul, 2 * width * features),
        )(error, *parts, *held)

    dec_grad = dec_grad_slot(0, BLOCKS, own)

    def pieces_of(masks, own_half, arrived):
        return pl.pallas_call(
            functools.partial(sum_kernel, masks),
            name="sum",
            out_shape=tuple(struct((tok, own_features), F32 if mask == 0 else BF16) for mask in masks),
            in_specs=[*vmem(2), pl.BlockSpec(memory_space=pl.ANY)],
            out_specs=tuple(vmem(len(masks))),
            compiler_params=params(2),
            cost_estimate=cost(tok * features, 2 * MIB),
        )(own_half, arrived, dec_grad)

    grads = {}
    for masks, own_half, arrived in ((FAR, own_far, arrived_far), (NEAR, own_near, arrived_near)):
        for mask, piece in zip(masks, pieces_of(masks, own_half, arrived)):
            grads[mask] = exchanged(piece, mask) if mask else piece
    dec_grad = dec_grad_slot(1, BLOCKS, previous, dec_grad)

    block = 128 if own_features % 128 == 0 else own_features
    enc_grad = pl.pallas_call(
        enc_grad_kernel,
        name="enc_grad",
        grid=(own_features // block,),
        out_shape=struct(enc_w.shape, BF16),
        in_specs=[
            *[pl.BlockSpec((tok, block), lambda j: (0, j))] * count,
            *[pl.BlockSpec((tok, width), lambda j: (0, 0))] * count,
            pl.BlockSpec((tok, block), lambda j: (0, j)),
        ],
        out_specs=pl.BlockSpec((1, block, model), lambda j: (0, j, 0)),
        compiler_params=params(16),
        cost_estimate=cost(matmul, 2 * own_features * model),
    )(*[grads[mask] for mask in MASKS], *inputs_of, active)
    return enc_grad, dec_grad


def plain(inputs, targets, enc_w, enc_b, dec_w, dec_b):
    scale = inputs.shape[1] ** (-0.5)
    gathered = lax.all_gather(inputs[0], "feat", axis=1, tiled=True)
    active = jnp.maximum(against(gathered, enc_w[0]) + enc_b[0], 0.0)
    codes = (active * active).astype(BF16)
    own = lax.all_gather(codes, "feat", axis=1, tiled=True)
    previous = from_behind(own, "section", 1)
    weights = dec_w[0]
    total = dec_b[0] + against(own, weights[0]) + against(previous, weights[1])
    error = ((total - targets[0].astype(F32)) * scale).astype(BF16)
    sent = jnp.dot(error, weights[1], preferred_element_type=F32)
    code_grad = jnp.dot(error, weights[0], preferred_element_type=F32) + from_behind(sent, "section", -1)
    mine = lax.psum_scatter(code_grad, "feat", scatter_dimension=1, tiled=True)
    pre_grad = (mine * 2.0 * active).astype(BF16)
    enc_grad = transposed(pre_grad, gathered).astype(BF16)[None]
    dec_grad = jnp.stack([transposed(error, source).astype(BF16) for source in (own, previous)])[None]
    return enc_grad, dec_grad


def chosen(inputs, targets, enc_w, enc_b, dec_w, dec_b):
    aligned = all(size % LANES == 0 for size in (*inputs.shape[1:], enc_w.shape[1]))
    fits = lax.axis_size("feat") == len(MASKS) and dec_w.shape[1] == 2
    body = on_device if aligned and fits else plain
    return body(inputs, targets, enc_w, enc_b, dec_w, dec_b)


def solution(mesh):
    return jax.shard_map(
        chosen,
        mesh=mesh,
        in_specs=(
            P("section", None, "feat"),
            P("section", None, "feat"),
            P("section", "feat", None),
            P("section", "feat"),
            P("section", None, "feat", None),
            P("section", "feat"),
        ),
        out_specs=(P("section", "feat", None), P("section", None, "feat", None)),
        check_vma=False,
    )
```

```python
import functools

import jax
import jax.numpy as jnp
from jax import lax
from jax.experimental import pallas as pl
from jax.experimental.pallas import tpu as pltpu
from jax.sharding import PartitionSpec as P

LANES = 128
MIB = 1024 * 1024
BF16 = jnp.bfloat16
F32 = jnp.float32

OFFSETS = (0, -1, 1, -2, 2, -3, 3, 4)
COUNT = len(OFFSETS)
BLOCKS = ((0,), (1, 2, 3), (6, 4), (7, 5))


def from_behind(value, axis, steps):
    count = lax.axis_size(axis)
    initial, last = (max(0, -steps), min(count, count - steps))
    return lax.ppermute(value, axis, [(source, source + steps) for source in range(initial, last)])


def transposed(left, right):
    return lax.dot_general(left, right, (((0,), (0,)), ((), ())), preferred_element_type=F32)


def against(left, right):
    return lax.dot_general(left, right, (((1,), (1,)), ((), ())), preferred_element_type=F32)


def exchanged(value, mask):
    count = lax.axis_size("feat")
    return lax.ppermute(value, "feat", [(i, i ^ mask) for i in range(count)])


def ring(count):
    return [*range(0, count, 2), *range(count - 1, 0, -2)]


def passed_on(value, by):
    count = lax.axis_size("feat")
    order = ring(count)
    return lax.ppermute(value, "feat", [(order[p], order[(p + by) % count]) for p in range(count)])


def ring_owner(offset):
    count = COUNT
    me = lax.axis_index("feat")
    half = me // 2
    place = jnp.where(lax.rem(me, 2) == 0, half, count - 1 - half)
    place = lax.rem(place + offset + count, count)
    return jnp.where(place < count // 2, 2 * place, 2 * (count - 1 - place) + 1)


def ring_gather(own):
    count = lax.axis_size("feat")
    middle = own.shape[0] // 2
    found = {0: (own[:middle], own[middle:])}
    first, last = ({0: part} for part in found[0])
    for step in range(1, count // 2):
        for held in (first, last):
            held[-step] = passed_on(held[1 - step], 1)
            held[step] = passed_on(held[step - 1], -1)
    far = count // 2
    first[far] = passed_on(first[1 - far], 1)
    last[far] = passed_on(last[far - 1], -1)
    return first, last


def owner(mask):
    return jnp.bitwise_xor(lax.axis_index("feat"), mask)


def columns(index, width):
    return pl.ds(pl.multiple_of(index * width, width), width)


def vmem(count):
    return [pl.BlockSpec(memory_space=pltpu.VMEM)] * count


def params(mib):
    return pltpu.CompilerParams(vmem_limit_bytes=mib * MIB)


def flat(groups):
    return [(i, row, mask) for i, masks in enumerate(groups) for row, mask in enumerate(masks)]


def pack_kernel(count, *refs):
    out_ref, start = refs[-1], 0
    for ref in refs[:count]:
        out_ref[start : start + ref.shape[0], :] = ref[...]
        start += ref.shape[0]


def packed(parts, after=()):
    rows = sum(part.shape[0] for part in parts)
    return pl.pallas_call(
        functools.partial(pack_kernel, len(parts)),
        name="pack",
        out_shape=jax.ShapeDtypeStruct((rows, parts[0].shape[1]), parts[0].dtype),
        in_specs=[*vmem(len(parts)), *[pl.BlockSpec(memory_space=pl.ANY) for _ in after]],
        out_specs=vmem(1)[0],
        compiler_params=params(1),
        cost_estimate=pl.CostEstimate(
            flops=0, bytes_accessed=4 * rows * parts[0].shape[1], transcendentals=0
        ),
    )(*parts, *after)


def block(parts, k):
    return jnp.concatenate([parts[2 * k][...], parts[2 * k + 1][...]], axis=0)


def pre_kernel(*refs):
    count = len(OFFSETS)
    parts, (w_ref, b_ref, codes_ref, active_ref, held, sems) = refs[: 2 * count], refs[2 * count :]
    width = parts[0].shape[1]
    copies = [
        pltpu.make_async_copy(w_ref.at[:, columns(ring_owner(offset), width)], held.at[k], sems.at[k])
        for k, offset in enumerate(OFFSETS)
    ]
    for copy in copies:
        copy.start()
    total = None
    for k, copy in enumerate(copies):
        copy.wait()
        term = against(block(parts, k), held[k])
        total = term if total is None else total + term
    active = jnp.maximum(total + b_ref[...], 0.0)
    active_ref[...] = active
    codes_ref[...] = (active * active).astype(BF16)


def row_copies(source, slot, target, sems):
    steps, tile = tiles(target.shape[0])
    return [
        pltpu.make_async_copy(
            source.at[slot, j * tile : (j + 1) * tile, :], target.at[j * tile : (j + 1) * tile, :], sems.at[j]
        )
        for j in range(steps)
    ]


def decoded(w_ref, here, parts, groups, tok, total):
    width = parts[0].shape[1]
    for i, row, mask in flat(groups):
        part = parts[i][row * tok : (row + 1) * tok, :]
        term = against(w_ref[here, columns(owner(mask), width)], part)
        total = term if total is None else total + term
    return total


def tiles(size):
    tile = 256 if size % 256 == 0 else LANES
    return size // tile, tile


def own_recon_kernel(*refs):
    parts, (w_ref, total_ref, held_ref, sems) = refs[: len(BLOCKS)], refs[len(BLOCKS) :]
    tok = total_ref.shape[1]
    _, tile = tiles(held_ref.shape[0])
    copies = row_copies(w_ref, 0, held_ref, sems)
    for copy in copies:
        copy.start()
    for j, copy in enumerate(copies):
        copy.wait()
        here = slice(j * tile, (j + 1) * tile)
        total_ref[here, :] = decoded(held_ref, here, parts, BLOCKS, tok, None)


def product(error_ref, w_ref, out_ref, first):
    wide = out_ref.shape[1]
    steps, tile = (wide // 512, 512) if wide % 512 == 0 else (wide // LANES, LANES)

    @pl.loop(0, steps)
    def _(j):
        source = pl.ds(pl.multiple_of(first * wide + j * tile, tile), tile)
        here = pl.ds(pl.multiple_of(j * tile, tile), tile)
        out_ref[:, here] = jnp.dot(
            error_ref[...], w_ref[:, source], preferred_element_type=F32
        ).astype(out_ref.dtype)


def halves():
    near = lax.axis_index("feat") // (COUNT // 2)
    return near, 1 - near


def recon_kernel(scale, *refs):
    parts = refs[: len(BLOCKS)]
    total_ref, w_ref, b_ref, target_ref, error_ref, far_ref, held_ref, sems = refs[len(BLOCKS) :]
    tok = total_ref.shape[1]
    _, tile = tiles(held_ref.shape[0])
    copies = row_copies(w_ref, 1, held_ref, sems)
    for copy in copies:
        copy.start()
    for j, copy in enumerate(copies):
        copy.wait()
        here = slice(j * tile, (j + 1) * tile)
        total = decoded(held_ref, here, parts, BLOCKS, tok, total_ref[here, :])
        error = total.T + b_ref[:, here] - target_ref[:, here].astype(F32)
        error_ref[:, here] = (error * scale).astype(BF16)
    product(error_ref, held_ref, far_ref, halves()[1])


def own_grad_kernel(error_ref, own_ref, next_ref, sent_ref, near_ref, far_ref):
    near, far = halves()
    product(error_ref, next_ref, sent_ref, near)
    product(error_ref, own_ref, far_ref, far)
    product(error_ref, own_ref, near_ref, near)


def dec_grad_kernel(groups, *refs):
    error_ref, parts, out_ref = refs[0], refs[1 : 1 + len(groups)], refs[-1]
    width = parts[0].shape[1]
    tok = error_ref.shape[0]
    for i, row, mask in flat(groups):
        part = parts[i][row * tok : (row + 1) * tok, :]
        out_ref[0, 0, :, columns(owner(mask), width)] = transposed(error_ref[...], part).astype(BF16)


def sum_kernel(groups, own_ref, arrived_ref, *outs):
    width = outs[0].shape[1]
    tok = own_ref.shape[0]
    for i, row, mask in flat(groups):
        here = columns(lax.rem(owner(mask), COUNT // 2), width)
        total = own_ref[:, here] + arrived_ref[:, here].astype(F32)
        outs[i][row * tok : (row + 1) * tok, :] = total.astype(outs[i].dtype)


def add_kernel(kept_ref, arrived_ref, *outs):
    tok = outs[0].shape[0]
    for row, out_ref in enumerate(outs):
        here = slice(row * tok, (row + 1) * tok)
        out_ref[...] = (kept_ref[here, :] + arrived_ref[here, :].astype(F32)).astype(out_ref.dtype)


def enc_grad_kernel(*refs):
    grads, parts = refs[: -2 - 2 * COUNT], refs[-2 - 2 * COUNT : -2]
    active_ref, out_ref = refs[-2:]
    width = parts[0].shape[1]
    total = grads[0][...]
    for grad in grads[1:]:
        total = total + grad[...].astype(F32)
    pre_grad = (total * 2.0 * active_ref[...]).astype(BF16)
    for k, offset in enumerate(OFFSETS):
        out_ref[0, :, columns(ring_owner(offset), width)] = transposed(pre_grad, block(parts, k)).astype(BF16)


def cost(flops, moved):
    return pl.CostEstimate(flops=flops, bytes_accessed=moved, transcendentals=0)


def on_device(inputs, targets, enc_w, enc_b, dec_w, dec_b):
    count = COUNT
    tok, width = inputs.shape[1:]
    own_features, model = enc_w.shape[1:]
    features = dec_w.shape[3]
    scale = tok ** (-0.5)
    matmul = 2 * tok * width * features
    half = (tok, features // 2)
    struct = jax.ShapeDtypeStruct

    first, last = ring_gather(inputs[0])
    inputs_of = [part for offset in OFFSETS for part in (first[offset], last[offset])]
    enc_weights, weights = [pltpu.with_memory_space_constraint(w[0], pltpu.HBM) for w in (enc_w, dec_w)]

    codes, active = pl.pallas_call(
        pre_kernel,
        name="pre",
        out_shape=(struct((tok, own_features), BF16), struct((tok, own_features), F32)),
        in_specs=[*vmem(2 * count), pl.BlockSpec(memory_space=pltpu.HBM), *vmem(1)],
        out_specs=tuple(vmem(2)),
        scratch_shapes=[pltpu.VMEM((count, own_features, width), BF16), pltpu.SemaphoreType.DMA((count,))],
        compiler_params=params(20),
        cost_estimate=cost(2 * tok * own_features * model, 2 * own_features * model),
    )(*inputs_of, enc_weights, enc_b)

    near_line = exchanged(codes, 2)
    across = exchanged(codes, 1)
    far_line = exchanged(codes, 6)
    farther_line = exchanged(codes, 4)
    near_across = exchanged(codes, 3)
    near_three = packed((across, near_line, near_across))
    previous_codes = from_behind(codes, "section", 1)
    previous_near = from_behind(near_three, "section", 1)
    far_pair = packed((far_line, farther_line), (previous_codes, near_three))
    far_across = exchanged(far_pair, 1)
    own = [codes, near_three, far_pair, far_across]
    previous = [
        previous_codes,
        previous_near,
        from_behind(far_pair, "section", 1),
        from_behind(far_across, "section", 1),
    ]

    held = pltpu.VMEM((width, features), BF16)
    sems = [pltpu.SemaphoreType.DMA((tiles(width)[0],))]
    total, own_weights = pl.pallas_call(
        own_recon_kernel,
        name="own_recon",
        out_shape=(struct((width, tok), F32), held),
        in_specs=[*vmem(len(own)), pl.BlockSpec(memory_space=pltpu.HBM)],
        out_specs=tuple(vmem(2)),
        scratch_shapes=sems,
        compiler_params=params(8),
        cost_estimate=cost(matmul, 4 * MIB),
    )(*own, weights)

    error, sent_far, next_weights = pl.pallas_call(
        functools.partial(recon_kernel, scale),
        name="recon",
        out_shape=(struct((tok, width), BF16), struct(half, BF16), held),
        in_specs=[*vmem(len(previous) + 1), pl.BlockSpec(memory_space=pltpu.HBM), *vmem(2)],
        out_specs=tuple(vmem(3)),
        scratch_shapes=sems,
        compiler_params=params(8),
        cost_estimate=cost(2 * matmul, 4 * MIB),
    )(*previous, total, weights, dec_b, targets[0])
    arrived_far = from_behind(sent_far, "section", -1)

    sent_near, own_near, own_far = pl.pallas_call(
        own_grad_kernel,
        name="own_grad",
        out_shape=(struct(half, BF16), struct(half, F32), struct(half, F32)),
        in_specs=vmem(3),
        out_specs=tuple(vmem(3)),
        compiler_params=params(8),
        cost_estimate=cost(3 * matmul // 2, 6 * MIB),
    )(error, own_weights, next_weights)
    arrived_near = from_behind(sent_near, "section", -1)

    rows = 256 if width % 256 == 0 else LANES

    def dec_grad_slot(slot, groups, parts, *held):
        return pl.pallas_call(
            functools.partial(dec_grad_kernel, groups),
            name="dec_grad",
            grid=(width // rows,),
            out_shape=struct(dec_w.shape, BF16),
            in_specs=[
                pl.BlockSpec((tok, rows), lambda j: (0, j)),
                *[pl.BlockSpec(part.shape, lambda j: (0, 0)) for part in parts],
                *[pl.BlockSpec(memory_space=pltpu.HBM) for _ in held],
            ],
            out_specs=pl.BlockSpec((1, 1, rows, features), lambda j: (0, slot, j, 0)),
            input_output_aliases={1 + len(parts): 0} if held else {},
            compiler_params=params(12),
            cost_estimate=cost(matmul, 2 * width * features),
        )(error, *parts, *held)

    dec_grad = dec_grad_slot(0, BLOCKS, own)

    def sums(groups, kinds, own_half, arrived):
        return pl.pallas_call(
            functools.partial(sum_kernel, groups),
            name="sum",
            out_shape=tuple(struct((len(g) * tok, own_features), kind) for g, kind in zip(groups, kinds)),
            in_specs=vmem(2),
            out_specs=tuple(vmem(len(groups))),
            compiler_params=params(2),
            cost_estimate=cost(tok * features, 2 * MIB),
        )(own_half, arrived)

    kept, crossing = sums(((6, 4), (7, 5)), (F32, BF16), own_far, arrived_far)
    lines = pl.pallas_call(
        add_kernel,
        name="add",
        out_shape=(struct((tok, own_features), BF16),) * 2,
        in_specs=vmem(2),
        out_specs=tuple(vmem(2)),
        compiler_params=params(2),
        cost_estimate=cost(tok * own_features, MIB),
    )(kept, exchanged(crossing, 1))
    near_sums = sums(((0,), (1,), (2,), (3,)), (F32, BF16, BF16, BF16), own_near, arrived_near)
    grads = [
        near_sums[0],
        *[exchanged(near_sums[mask], mask) for mask in (1, 2, 3)],
        *[exchanged(line, mask) for mask, line in zip((6, 4), lines)],
    ]
    held_grad = pltpu.with_memory_space_constraint(dec_grad, pltpu.HBM)
    dec_grad = dec_grad_slot(1, BLOCKS, previous, held_grad)

    enc_grad = pl.pallas_call(
        enc_grad_kernel,
        name="enc_grad",
        grid=(own_features // LANES,),
        out_shape=struct(enc_w.shape, BF16),
        in_specs=[
            *[pl.BlockSpec((tok, LANES), lambda j: (0, j))] * len(grads),
            *[pl.BlockSpec((tok // 2, width), lambda j: (0, 0))] * (2 * count),
            pl.BlockSpec((tok, LANES), lambda j: (0, j)),
        ],
        out_specs=pl.BlockSpec((1, LANES, model), lambda j: (0, j, 0)),
        compiler_params=params(16),
        cost_estimate=cost(matmul, 2 * own_features * model),
    )(*grads, *inputs_of, active)
    return enc_grad, dec_grad


def plain(inputs, targets, enc_w, enc_b, dec_w, dec_b):
    scale = inputs.shape[1] ** (-0.5)
    gathered = lax.all_gather(inputs[0], "feat", axis=1, tiled=True)
    active = jnp.maximum(against(gathered, enc_w[0]) + enc_b[0], 0.0)
    codes = (active * active).astype(BF16)
    own = lax.all_gather(codes, "feat", axis=1, tiled=True)
    previous = from_behind(own, "section", 1)
    weights = dec_w[0]
    total = dec_b[0] + against(own, weights[0]) + against(previous, weights[1])
    error = ((total - targets[0].astype(F32)) * scale).astype(BF16)
    sent = jnp.dot(error, weights[1], preferred_element_type=F32)
    code_grad = jnp.dot(error, weights[0], preferred_element_type=F32) + from_behind(sent, "section", -1)
    mine = lax.psum_scatter(code_grad, "feat", scatter_dimension=1, tiled=True)
    pre_grad = (mine * 2.0 * active).astype(BF16)
    enc_grad = transposed(pre_grad, gathered).astype(BF16)[None]
    dec_grad = jnp.stack([transposed(error, source).astype(BF16) for source in (own, previous)])[None]
    return enc_grad, dec_grad


def chosen(inputs, targets, enc_w, enc_b, dec_w, dec_b):
    aligned = all(size % LANES == 0 for size in (*inputs.shape[1:], enc_w.shape[1]))
    fits = lax.axis_size("feat") == COUNT and dec_w.shape[1] == 2
    body = on_device if aligned and fits else plain
    return body(inputs, targets, enc_w, enc_b, dec_w, dec_b)


def solution(mesh):
    return jax.shard_map(
        chosen,
        mesh=mesh,
        in_specs=(
            P("section", None, "feat"),
            P("section", None, "feat"),
            P("section", "feat", None),
            P("section", "feat"),
            P("section", None, "feat", None),
            P("section", "feat"),
        ),
        out_specs=(P("section", "feat", None), P("section", None, "feat", None)),
        check_vma=False,
    )
```

```python
import functools

import jax
import jax.numpy as jnp
from jax import lax
from jax.experimental import pallas as pl
from jax.experimental.pallas import tpu as pltpu
from jax.sharding import PartitionSpec as P

LANES = 128
MIB = 1024 * 1024
BF16 = jnp.bfloat16
F32 = jnp.float32

OFFSETS = (0, -1, 1, -2, 2, -3, 3, 4)
COUNT = len(OFFSETS)
NEAR = (0, 1, 2, 3)
FAR = (6, 4)
CROSSING = (7, 5)
BLOCKS = ((0, 1, 2, 3), (6, 4), (7, 5))


def from_behind(value, axis, steps):
    count = lax.axis_size(axis)
    initial, last = (max(0, -steps), min(count, count - steps))
    return lax.ppermute(value, axis, [(source, source + steps) for source in range(initial, last)])


def transposed(left, right):
    return lax.dot_general(left, right, (((0,), (0,)), ((), ())), preferred_element_type=F32)


def against(left, right):
    return lax.dot_general(left, right, (((1,), (1,)), ((), ())), preferred_element_type=F32)


def exchanged(value, mask):
    count = lax.axis_size("feat")
    return lax.ppermute(value, "feat", [(i, i ^ mask) for i in range(count)])


def ring(count):
    return [*range(0, count, 2), *range(count - 1, 0, -2)]


def passed_on(value, by):
    count = lax.axis_size("feat")
    order = ring(count)
    return lax.ppermute(value, "feat", [(order[p], order[(p + by) % count]) for p in range(count)])


def ring_owner(offset):
    count = COUNT
    me = lax.axis_index("feat")
    half = me // 2
    place = jnp.where(lax.rem(me, 2) == 0, half, count - 1 - half)
    place = lax.rem(place + offset + count, count)
    return jnp.where(place < count // 2, 2 * place, 2 * (count - 1 - place) + 1)


def ring_gather(own):
    count = lax.axis_size("feat")
    middle = own.shape[0] // 2
    found = {0: (own[:middle], own[middle:])}
    first, last = ({0: part} for part in found[0])
    for step in range(1, count // 2):
        for held in (first, last):
            held[-step] = passed_on(held[1 - step], 1)
            held[step] = passed_on(held[step - 1], -1)
    far = count // 2
    first[far] = passed_on(first[1 - far], 1)
    last[far] = passed_on(last[far - 1], -1)
    return first, last


def owner(mask):
    return jnp.bitwise_xor(lax.axis_index("feat"), mask)


def columns(index, width):
    return pl.ds(pl.multiple_of(index * width, width), width)


def vmem(count):
    return [pl.BlockSpec(memory_space=pltpu.VMEM)] * count


def params(mib):
    return pltpu.CompilerParams(vmem_limit_bytes=mib * MIB)


def flat(groups):
    return [(i, row, mask) for i, masks in enumerate(groups) for row, mask in enumerate(masks)]


def pack_kernel(*refs):
    out_ref, start = refs[-1], 0
    for ref in refs[:-1]:
        out_ref[start : start + ref.shape[0], :] = ref[...]
        start += ref.shape[0]


def packed(*parts):
    rows = sum(part.shape[0] for part in parts)
    return pl.pallas_call(
        pack_kernel,
        name="pack",
        out_shape=jax.ShapeDtypeStruct((rows, parts[0].shape[1]), parts[0].dtype),
        in_specs=vmem(len(parts)),
        out_specs=vmem(1)[0],
        compiler_params=params(1),
        cost_estimate=pl.CostEstimate(
            flops=0, bytes_accessed=4 * rows * parts[0].shape[1], transcendentals=0
        ),
    )(*parts)


def block(parts, k):
    return jnp.concatenate([parts[2 * k][...], parts[2 * k + 1][...]], axis=0)


def in_turn(copies, ahead):
    for copy in copies[:ahead]:
        copy.start()
    for k, copy in enumerate(copies):
        copy.wait()
        for later in copies[k + ahead : k + ahead + 1]:
            later.start()
        yield k


def pre_kernel(*refs):
    count = len(OFFSETS)
    parts, (w_ref, b_ref, codes_ref, active_ref, held, bias, sems) = refs[: 2 * count], refs[2 * count :]
    width = parts[0].shape[1]
    copies = [
        pltpu.make_async_copy(w_ref.at[:, columns(ring_owner(offset), width)], held.at[k], sems.at[k])
        for k, offset in enumerate(OFFSETS)
    ]
    bias_copy = pltpu.make_async_copy(b_ref, bias, sems.at[count])
    bias_copy.start()
    total = None
    for k in in_turn(copies, 3):
        term = against(block(parts, k), held[k])
        total = term if total is None else total + term
    bias_copy.wait()
    active = jnp.maximum(total + bias[...], 0.0)
    active_ref[...] = active
    codes_ref[...] = (active * active).astype(BF16)


def row_copies(source, slot, target, sems):
    steps, tile = tiles(target.shape[0])
    return [
        pltpu.make_async_copy(
            source.at[slot, j * tile : (j + 1) * tile, :], target.at[j * tile : (j + 1) * tile, :], sems.at[j]
        )
        for j in range(steps)
    ]


def decoded(w_ref, here, parts, groups, tok, total):
    width = parts[0].shape[1]
    for i, row, mask in flat(groups):
        part = parts[i][row * tok : (row + 1) * tok, :]
        term = against(w_ref[here, columns(owner(mask), width)], part)
        total = term if total is None else total + term
    return total


def tiles(size):
    tile = 256 if size % 256 == 0 else LANES
    return size // tile, tile


def own_recon_kernel(*refs):
    parts, (w_ref, total_ref, held_ref, sems) = refs[: len(BLOCKS)], refs[len(BLOCKS) :]
    tok = total_ref.shape[1]
    _, tile = tiles(held_ref.shape[0])
    copies = row_copies(w_ref, 0, held_ref, sems)
    for j in in_turn(copies, 2):
        here = slice(j * tile, (j + 1) * tile)
        total_ref[here, :] = decoded(held_ref, here, parts, BLOCKS, tok, None)


def products(error_ref, w_ref, masks, out_ref):
    tok = error_ref.shape[0]
    for row, mask in enumerate(masks):
        term = jnp.dot(
            error_ref[...], w_ref[:, columns(owner(mask), out_ref.shape[1])], preferred_element_type=F32
        )
        out_ref[row * tok : (row + 1) * tok, :] = term.astype(out_ref.dtype)


def recon_kernel(scale, *refs):
    parts = refs[: len(BLOCKS)]
    total_ref, w_ref, b_ref, target_ref, error_ref, far_ref, held_ref, sems = refs[len(BLOCKS) :]
    tok = total_ref.shape[1]
    _, tile = tiles(held_ref.shape[0])
    copies = row_copies(w_ref, 1, held_ref, sems)
    for j in in_turn(copies, 2):
        here = slice(j * tile, (j + 1) * tile)
        total = decoded(held_ref, here, parts, BLOCKS, tok, total_ref[here, :])
        error = total.T + b_ref[:, here] - target_ref[:, here].astype(F32)
        error_ref[:, here] = (error * scale).astype(BF16)
    products(error_ref, held_ref, FAR + CROSSING, far_ref)


def own_grad_kernel(error_ref, own_ref, next_ref, sent_ref, near_ref, far_ref):
    products(error_ref, next_ref, NEAR, sent_ref)
    products(error_ref, own_ref, FAR + CROSSING, far_ref)
    products(error_ref, own_ref, NEAR, near_ref)


def dec_grad_kernel(groups, *refs):
    error_ref, parts, out_ref = refs[0], refs[1 : 1 + len(groups)], refs[-1]
    width = parts[0].shape[1]
    tok = error_ref.shape[0]
    for i, row, mask in flat(groups):
        part = parts[i][row * tok : (row + 1) * tok, :]
        out_ref[0, 0, :, columns(owner(mask), width)] = transposed(error_ref[...], part).astype(BF16)


def add_kernel(own_ref, arrived_ref, *outs):
    first = 0
    for out_ref in outs:
        here = slice(first, first + out_ref.shape[0])
        out_ref[...] = (own_ref[here, :] + arrived_ref[here, :].astype(F32)).astype(out_ref.dtype)
        first += out_ref.shape[0]


def enc_grad_kernel(*refs):
    grads, parts = refs[: -2 - 2 * COUNT], refs[-2 - 2 * COUNT : -2]
    active_ref, out_ref = refs[-2:]
    width = parts[0].shape[1]
    total = grads[0][...]
    for grad in grads[1:]:
        total = total + grad[...].astype(F32)
    pre_grad = (total * 2.0 * active_ref[...]).astype(BF16)
    for k, offset in enumerate(OFFSETS):
        out_ref[0, :, columns(ring_owner(offset), width)] = transposed(pre_grad, block(parts, k)).astype(BF16)


def cost(flops, moved):
    return pl.CostEstimate(flops=flops, bytes_accessed=moved, transcendentals=0)


def on_device(inputs, targets, enc_w, enc_b, dec_w, dec_b):
    count = COUNT
    tok, width = inputs.shape[1:]
    own_features, model = enc_w.shape[1:]
    features = dec_w.shape[3]
    scale = tok ** (-0.5)
    matmul = 2 * tok * width * features
    struct = jax.ShapeDtypeStruct

    def stack(masks, kind):
        return struct((len(masks) * tok, own_features), kind)


    first, last = ring_gather(inputs[0])
    inputs_of = [part for offset in OFFSETS for part in (first[offset], last[offset])]
    enc_weights, weights = [pltpu.with_memory_space_constraint(w[0], pltpu.HBM) for w in (enc_w, dec_w)]

    codes, active = pl.pallas_call(
        pre_kernel,
        name="pre",
        out_shape=(struct((tok, own_features), BF16), struct((tok, own_features), F32)),
        in_specs=[*vmem(2 * count), *[pl.BlockSpec(memory_space=pltpu.HBM)] * 2],
        out_specs=tuple(vmem(2)),
        scratch_shapes=[
            pltpu.VMEM((count, own_features, width), BF16),
            pltpu.VMEM(enc_b.shape, F32),
            pltpu.SemaphoreType.DMA((count + 1,)),
        ],
        compiler_params=params(20),
        cost_estimate=cost(2 * tok * own_features * model, 2 * own_features * model),
    )(*inputs_of, enc_weights, pltpu.with_memory_space_constraint(enc_b, pltpu.HBM))

    far_pair = packed(exchanged(codes, 6), exchanged(codes, 4))
    far_across = exchanged(far_pair, 1)
    own = [packed(codes, *[exchanged(codes, mask) for mask in (1, 2, 3)]), far_pair, far_across]
    previous = [from_behind(part, "section", 1) for part in own]

    held = pltpu.VMEM((width, features), BF16)
    sems = [pltpu.SemaphoreType.DMA((tiles(width)[0],))]
    total, own_weights = pl.pallas_call(
        own_recon_kernel,
        name="own_recon",
        out_shape=(struct((width, tok), F32), held),
        in_specs=[*vmem(len(own)), pl.BlockSpec(memory_space=pltpu.HBM)],
        out_specs=tuple(vmem(2)),
        scratch_shapes=sems,
        compiler_params=params(8),
        cost_estimate=cost(matmul, 4 * MIB),
    )(*own, weights)

    error, sent_far, next_weights = pl.pallas_call(
        functools.partial(recon_kernel, scale),
        name="recon",
        out_shape=(struct((tok, width), BF16), stack(FAR + CROSSING, BF16), held),
        in_specs=[*vmem(len(previous) + 1), pl.BlockSpec(memory_space=pltpu.HBM), *vmem(2)],
        out_specs=tuple(vmem(3)),
        scratch_shapes=sems,
        compiler_params=params(8),
        cost_estimate=cost(2 * matmul, 4 * MIB),
    )(*previous, total, weights, dec_b, targets[0])
    arrived_far = from_behind(sent_far, "section", -1)

    sent_near, own_near, own_far = pl.pallas_call(
        own_grad_kernel,
        name="own_grad",
        out_shape=(stack(NEAR, BF16), stack(NEAR, F32), stack(FAR + CROSSING, F32)),
        in_specs=vmem(3),
        out_specs=tuple(vmem(3)),
        compiler_params=params(8),
        cost_estimate=cost(3 * matmul // 2, 6 * MIB),
    )(error, own_weights, next_weights)
    arrived_near = from_behind(sent_near, "section", -1)

    rows = 256 if width % 256 == 0 else LANES

    def dec_grad_slot(slot, groups, parts, *held):
        return pl.pallas_call(
            functools.partial(dec_grad_kernel, groups),
            name="dec_grad",
            grid=(width // rows,),
            out_shape=struct(dec_w.shape, BF16),
            in_specs=[
                pl.BlockSpec((tok, rows), lambda j: (0, j)),
                *[pl.BlockSpec(part.shape, lambda j: (0, 0)) for part in parts],
                *[pl.BlockSpec(memory_space=pltpu.HBM) for _ in held],
            ],
            out_specs=pl.BlockSpec((1, 1, rows, features), lambda j: (0, slot, j, 0)),
            input_output_aliases={1 + len(parts): 0} if held else {},
            compiler_params=params(12),
            cost_estimate=cost(matmul, 2 * width * features),
        )(error, *parts, *held)

    dec_grad = dec_grad_slot(0, BLOCKS, own)

    def sums(outs, own_part, arrived):
        return pl.pallas_call(
            add_kernel,
            name="sum",
            out_shape=tuple(stack(masks, kind) for masks, kind in outs),
            in_specs=vmem(2),
            out_specs=tuple(vmem(len(outs))),
            compiler_params=params(2),
            cost_estimate=cost(tok * features, 2 * MIB),
        )(own_part, arrived)

    kept, crossing = sums(((FAR, F32), (CROSSING, BF16)), own_far, arrived_far)
    lines = sums([((mask,), BF16) for mask in FAR], kept, exchanged(crossing, 1))
    near = sums([((mask,), BF16 if mask else F32) for mask in NEAR], own_near, arrived_near)
    grads = [
        near[0],
        *[exchanged(near[mask], mask) for mask in NEAR[1:]],
        *[exchanged(line, mask) for mask, line in zip(FAR, lines)],
    ]
    held_grad = pltpu.with_memory_space_constraint(dec_grad, pltpu.HBM)
    dec_grad = dec_grad_slot(1, BLOCKS, previous, held_grad)

    enc_grad = pl.pallas_call(
        enc_grad_kernel,
        name="enc_grad",
        grid=(own_features // LANES,),
        out_shape=struct(enc_w.shape, BF16),
        in_specs=[
            *[pl.BlockSpec((tok, LANES), lambda j: (0, j))] * len(grads),
            *[pl.BlockSpec((tok // 2, width), lambda j: (0, 0))] * (2 * count),
            pl.BlockSpec((tok, LANES), lambda j: (0, j)),
        ],
        out_specs=pl.BlockSpec((1, LANES, model), lambda j: (0, j, 0)),
        compiler_params=params(16),
        cost_estimate=cost(matmul, 2 * own_features * model),
    )(*grads, *inputs_of, active)
    return enc_grad, dec_grad


def plain(inputs, targets, enc_w, enc_b, dec_w, dec_b):
    scale = inputs.shape[1] ** (-0.5)
    gathered = lax.all_gather(inputs[0], "feat", axis=1, tiled=True)
    active = jnp.maximum(against(gathered, enc_w[0]) + enc_b[0], 0.0)
    codes = (active * active).astype(BF16)
    own = lax.all_gather(codes, "feat", axis=1, tiled=True)
    previous = from_behind(own, "section", 1)
    weights = dec_w[0]
    total = dec_b[0] + against(own, weights[0]) + against(previous, weights[1])
    error = ((total - targets[0].astype(F32)) * scale).astype(BF16)
    sent = jnp.dot(error, weights[1], preferred_element_type=F32)
    code_grad = jnp.dot(error, weights[0], preferred_element_type=F32) + from_behind(sent, "section", -1)
    mine = lax.psum_scatter(code_grad, "feat", scatter_dimension=1, tiled=True)
    pre_grad = (mine * 2.0 * active).astype(BF16)
    enc_grad = transposed(pre_grad, gathered).astype(BF16)[None]
    dec_grad = jnp.stack([transposed(error, source).astype(BF16) for source in (own, previous)])[None]
    return enc_grad, dec_grad


def chosen(inputs, targets, enc_w, enc_b, dec_w, dec_b):
    aligned = all(size % LANES == 0 for size in (*inputs.shape[1:], enc_w.shape[1]))
    fits = lax.axis_size("feat") == COUNT and dec_w.shape[1] == 2
    body = on_device if aligned and fits else plain
    return body(inputs, targets, enc_w, enc_b, dec_w, dec_b)


def solution(mesh):
    return jax.shard_map(
        chosen,
        mesh=mesh,
        in_specs=(
            P("section", None, "feat"),
            P("section", None, "feat"),
            P("section", "feat", None),
            P("section", "feat"),
            P("section", None, "feat", None),
            P("section", "feat"),
        ),
        out_specs=(P("section", "feat", None), P("section", None, "feat", None)),
        check_vma=False,
    )
```

```python
import functools

import jax
import jax.numpy as jnp
from jax import lax
from jax.experimental import pallas as pl
from jax.experimental.pallas import tpu as pltpu
from jax.sharding import PartitionSpec as P

LANES = 128
MIB = 1024 * 1024
BF16 = jnp.bfloat16
F32 = jnp.float32

SPLIT_FLOPS = 10**10

OFFSETS = (0, -1, 1, -2, 2, -3, 3, 4)
COUNT = len(OFFSETS)
NEAR = (0, 1, 2, 3)
FAR = (6, 4)
CROSSING = (7, 5)
BLOCKS = ((0, 1, 2, 3), (6, 4), (7, 5))


def from_behind(value, axis, steps):
    count = lax.axis_size(axis)
    initial, last = (max(0, -steps), min(count, count - steps))
    return lax.ppermute(value, axis, [(source, source + steps) for source in range(initial, last)])


def transposed(left, right):
    return lax.dot_general(left, right, (((0,), (0,)), ((), ())), preferred_element_type=F32)


def against(left, right):
    return lax.dot_general(left, right, (((1,), (1,)), ((), ())), preferred_element_type=F32)


def exchanged(value, mask):
    count = lax.axis_size("feat")
    return lax.ppermute(value, "feat", [(i, i ^ mask) for i in range(count)])


def ring(count):
    return [*range(0, count, 2), *range(count - 1, 0, -2)]


def passed_on(value, by):
    count = lax.axis_size("feat")
    order = ring(count)
    return lax.ppermute(value, "feat", [(order[p], order[(p + by) % count]) for p in range(count)])


def ring_owner(offset):
    count = COUNT
    me = lax.axis_index("feat")
    half = me // 2
    place = jnp.where(lax.rem(me, 2) == 0, half, count - 1 - half)
    place = lax.rem(place + offset + count, count)
    return jnp.where(place < count // 2, 2 * place, 2 * (count - 1 - place) + 1)


def split_kernel(in_ref, first_ref, last_ref):
    middle = first_ref.shape[0]
    first_ref[...] = in_ref[:middle, :]
    last_ref[...] = in_ref[middle:, :]


def ring_gather(own):
    count = lax.axis_size("feat")
    part = jax.ShapeDtypeStruct((own.shape[0] // 2, own.shape[1]), own.dtype)
    first, last = (
        {0: part}
        for part in pl.pallas_call(
            split_kernel,
            name="split",
            out_shape=(part, part),
            in_specs=vmem(1),
            out_specs=tuple(vmem(2)),
            compiler_params=params(2),
            cost_estimate=cost(SPLIT_FLOPS, 0),
        )(own)
    )
    for step in range(1, count // 2):
        for held in (first, last):
            held[-step] = passed_on(held[1 - step], 1)
            held[step] = passed_on(held[step - 1], -1)
    far = count // 2
    first[far] = passed_on(first[1 - far], 1)
    last[far] = passed_on(last[far - 1], -1)
    return first, last


def owner(mask):
    return jnp.bitwise_xor(lax.axis_index("feat"), mask)


def columns(index, width):
    return pl.ds(pl.multiple_of(index * width, width), width)


def vmem(count):
    return [pl.BlockSpec(memory_space=pltpu.VMEM)] * count


def params(mib):
    return pltpu.CompilerParams(vmem_limit_bytes=mib * MIB)


def flat(groups):
    return [(i, row, mask) for i, masks in enumerate(groups) for row, mask in enumerate(masks)]


def pack_kernel(*refs):
    out_ref, start = refs[-1], 0
    for ref in refs[:-1]:
        out_ref[start : start + ref.shape[0], :] = ref[...]
        start += ref.shape[0]


def packed(*parts):
    rows = sum(part.shape[0] for part in parts)
    return pl.pallas_call(
        pack_kernel,
        name="pack",
        out_shape=jax.ShapeDtypeStruct((rows, parts[0].shape[1]), parts[0].dtype),
        in_specs=vmem(len(parts)),
        out_specs=vmem(1)[0],
        compiler_params=params(1),
        cost_estimate=pl.CostEstimate(
            flops=0, bytes_accessed=4 * rows * parts[0].shape[1], transcendentals=0
        ),
    )(*parts)


def block(parts, k):
    return jnp.concatenate([parts[2 * k][...], parts[2 * k + 1][...]], axis=0)


def pre_kernel(*refs):
    count = len(OFFSETS)
    parts, (w_ref, b_ref, codes_ref, active_ref) = refs[: 2 * count], refs[2 * count :]
    width = parts[0].shape[1]
    steps, tile = tiles(w_ref.shape[0])
    for j in range(steps):
        here = slice(j * tile, (j + 1) * tile)
        total = None
        for k, offset in enumerate(OFFSETS):
            term = against(w_ref[here, columns(ring_owner(offset), width)], block(parts, k))
            total = term if total is None else total + term
        active = jnp.maximum(total.T + b_ref[:, here], 0.0)
        active_ref[:, here] = active
        codes_ref[:, here] = (active * active).astype(BF16)


def decoded(w_ref, slot, here, parts, groups, tok, total):
    width = parts[0].shape[1]
    for i, row, mask in flat(groups):
        part = parts[i][row * tok : (row + 1) * tok, :]
        term = against(w_ref[slot, here, columns(owner(mask), width)], part)
        total = term if total is None else total + term
    return total


def tiles(size):
    tile = 256 if size % 256 == 0 else LANES
    return size // tile, tile


def own_recon_kernel(*refs):
    parts, (w_ref, total_ref) = refs[: len(BLOCKS)], refs[len(BLOCKS) :]
    tok = total_ref.shape[1]
    steps, tile = tiles(w_ref.shape[1])

    for j in range(steps):
        here = slice(j * tile, (j + 1) * tile)
        total_ref[here, :] = decoded(w_ref, 0, here, parts, BLOCKS, tok, None)


def products(error_ref, w_ref, slot, masks, out_ref):
    tok = error_ref.shape[0]
    for row, mask in enumerate(masks):
        term = jnp.dot(
            error_ref[...], w_ref[slot, :, columns(owner(mask), out_ref.shape[1])], preferred_element_type=F32
        )
        out_ref[row * tok : (row + 1) * tok, :] = term.astype(out_ref.dtype)


def recon_kernel(scale, *refs):
    parts, (total_ref, w_ref, b_ref, target_ref, error_ref, far_ref) = refs[: len(BLOCKS)], refs[len(BLOCKS) :]
    tok = total_ref.shape[1]
    steps, tile = tiles(w_ref.shape[1])

    for j in range(steps):
        here = slice(j * tile, (j + 1) * tile)
        total = decoded(w_ref, 1, here, parts, BLOCKS, tok, total_ref[here, :])
        error = total.T + b_ref[:, here] - target_ref[:, here].astype(F32)
        error_ref[:, here] = (error * scale).astype(BF16)

    products(error_ref, w_ref, 1, FAR + CROSSING, far_ref)


def own_grad_kernel(error_ref, w_ref, sent_ref, near_ref, far_ref):
    products(error_ref, w_ref, 1, NEAR, sent_ref)
    products(error_ref, w_ref, 0, FAR + CROSSING, far_ref)
    products(error_ref, w_ref, 0, NEAR, near_ref)


def dec_grad_kernel(groups, *refs):
    error_ref, parts, out_ref = refs[0], refs[1 : 1 + len(groups)], refs[-1]
    width = parts[0].shape[1]
    tok = error_ref.shape[0]
    for i, row, mask in flat(groups):
        part = parts[i][row * tok : (row + 1) * tok, :]
        out_ref[0, 0, :, columns(owner(mask), width)] = transposed(error_ref[...], part).astype(BF16)


def add_kernel(own_ref, arrived_ref, *outs):
    first = 0
    for out_ref in outs:
        here = slice(first, first + out_ref.shape[0])
        out_ref[...] = (own_ref[here, :] + arrived_ref[here, :].astype(F32)).astype(out_ref.dtype)
        first += out_ref.shape[0]


def enc_grad_kernel(*refs):
    grads, parts = refs[: -2 - 2 * COUNT], refs[-2 - 2 * COUNT : -2]
    active_ref, out_ref = refs[-2:]
    width = parts[0].shape[1]
    total = grads[0][...]
    for grad in grads[1:]:
        total = total + grad[...].astype(F32)
    pre_grad = (total * 2.0 * active_ref[...]).astype(BF16)
    for k, offset in enumerate(OFFSETS):
        out_ref[0, :, columns(ring_owner(offset), width)] = transposed(pre_grad, block(parts, k)).astype(BF16)


def cost(flops, moved):
    return pl.CostEstimate(flops=flops, bytes_accessed=moved, transcendentals=0)


def on_device(inputs, targets, enc_w, enc_b, dec_w, dec_b):
    count = COUNT
    tok, width = inputs.shape[1:]
    own_features, model = enc_w.shape[1:]
    features = dec_w.shape[3]
    scale = tok ** (-0.5)
    matmul = 2 * tok * width * features
    struct = jax.ShapeDtypeStruct

    def stack(masks, kind):
        return struct((len(masks) * tok, own_features), kind)


    first, last = ring_gather(inputs[0])
    inputs_of = [part for offset in OFFSETS for part in (first[offset], last[offset])]
    enc_weights, weights = [pltpu.with_memory_space_constraint(w[0], pltpu.VMEM) for w in (enc_w, dec_w)]

    codes, active = pl.pallas_call(
        pre_kernel,
        name="pre",
        out_shape=(struct((tok, own_features), BF16), struct((tok, own_features), F32)),
        in_specs=vmem(2 * count + 2),
        out_specs=tuple(vmem(2)),
        compiler_params=params(16),
        cost_estimate=cost(2 * tok * own_features * model, 0),
    )(*inputs_of, enc_weights, enc_b)

    far_pair = packed(exchanged(codes, 6), exchanged(codes, 4))
    far_across = exchanged(far_pair, 1)
    own = [packed(codes, *[exchanged(codes, mask) for mask in (1, 2, 3)]), far_pair, far_across]
    previous = [from_behind(part, "section", 1) for part in own]

    total = pl.pallas_call(
        own_recon_kernel,
        name="own_recon",
        out_shape=struct((width, tok), F32),
        in_specs=vmem(len(own) + 1),
        out_specs=vmem(1)[0],
        compiler_params=params(8),
        cost_estimate=cost(matmul, 0),
    )(*own, weights)

    error, sent_far = pl.pallas_call(
        functools.partial(recon_kernel, scale),
        name="recon",
        out_shape=(struct((tok, width), BF16), stack(FAR + CROSSING, BF16)),
        in_specs=vmem(len(previous) + 4),
        out_specs=tuple(vmem(2)),
        compiler_params=params(8),
        cost_estimate=cost(2 * matmul, 4 * MIB),
    )(*previous, total, weights, dec_b, targets[0])
    arrived_far = from_behind(sent_far, "section", -1)

    sent_near, own_near, own_far = pl.pallas_call(
        own_grad_kernel,
        name="own_grad",
        out_shape=(stack(NEAR, BF16), stack(NEAR, F32), stack(FAR + CROSSING, F32)),
        in_specs=vmem(2),
        out_specs=tuple(vmem(3)),
        compiler_params=params(8),
        cost_estimate=cost(3 * matmul // 2, 6 * MIB),
    )(error, weights)
    arrived_near = from_behind(sent_near, "section", -1)

    rows = 256 if width % 256 == 0 else LANES

    def dec_grad_slot(slot, groups, parts, *held):
        return pl.pallas_call(
            functools.partial(dec_grad_kernel, groups),
            name="dec_grad",
            grid=(width // rows,),
            out_shape=struct(dec_w.shape, BF16),
            in_specs=[
                pl.BlockSpec((tok, rows), lambda j: (0, j)),
                *[pl.BlockSpec(part.shape, lambda j: (0, 0)) for part in parts],
                *[pl.BlockSpec(memory_space=pltpu.HBM) for _ in held],
            ],
            out_specs=pl.BlockSpec((1, 1, rows, features), lambda j: (0, slot, j, 0)),
            input_output_aliases={1 + len(parts): 0} if held else {},
            compiler_params=params(12),
            cost_estimate=cost(matmul, 2 * width * features),
        )(error, *parts, *held)

    dec_grad = dec_grad_slot(0, BLOCKS, own)

    def sums(outs, own_part, arrived):
        return pl.pallas_call(
            add_kernel,
            name="sum",
            out_shape=tuple(stack(masks, kind) for masks, kind in outs),
            in_specs=vmem(2),
            out_specs=tuple(vmem(len(outs))),
            compiler_params=params(2),
            cost_estimate=cost(tok * features, 2 * MIB),
        )(own_part, arrived)

    kept, crossing = sums(((FAR, F32), (CROSSING, BF16)), own_far, arrived_far)
    lines = sums([((mask,), BF16) for mask in FAR], kept, exchanged(crossing, 1))
    near = sums([((mask,), BF16 if mask else F32) for mask in NEAR], own_near, arrived_near)
    grads = [
        near[0],
        *[exchanged(near[mask], mask) for mask in NEAR[1:]],
        *[exchanged(line, mask) for mask, line in zip(FAR, lines)],
    ]
    held_grad = pltpu.with_memory_space_constraint(dec_grad, pltpu.HBM)
    dec_grad = dec_grad_slot(1, BLOCKS, previous, held_grad)

    enc_grad = pl.pallas_call(
        enc_grad_kernel,
        name="enc_grad",
        grid=(own_features // LANES,),
        out_shape=struct(enc_w.shape, BF16),
        in_specs=[
            *[pl.BlockSpec((tok, LANES), lambda j: (0, j))] * len(grads),
            *[pl.BlockSpec((tok // 2, width), lambda j: (0, 0))] * (2 * count),
            pl.BlockSpec((tok, LANES), lambda j: (0, j)),
        ],
        out_specs=pl.BlockSpec((1, LANES, model), lambda j: (0, j, 0)),
        compiler_params=params(16),
        cost_estimate=cost(matmul, 2 * own_features * model),
    )(*grads, *inputs_of, active)
    return enc_grad, dec_grad


def plain(inputs, targets, enc_w, enc_b, dec_w, dec_b):
    scale = inputs.shape[1] ** (-0.5)
    gathered = lax.all_gather(inputs[0], "feat", axis=1, tiled=True)
    active = jnp.maximum(against(gathered, enc_w[0]) + enc_b[0], 0.0)
    codes = (active * active).astype(BF16)
    own = lax.all_gather(codes, "feat", axis=1, tiled=True)
    previous = from_behind(own, "section", 1)
    weights = dec_w[0]
    total = dec_b[0] + against(own, weights[0]) + against(previous, weights[1])
    error = ((total - targets[0].astype(F32)) * scale).astype(BF16)
    sent = jnp.dot(error, weights[1], preferred_element_type=F32)
    code_grad = jnp.dot(error, weights[0], preferred_element_type=F32) + from_behind(sent, "section", -1)
    mine = lax.psum_scatter(code_grad, "feat", scatter_dimension=1, tiled=True)
    pre_grad = (mine * 2.0 * active).astype(BF16)
    enc_grad = transposed(pre_grad, gathered).astype(BF16)[None]
    dec_grad = jnp.stack([transposed(error, source).astype(BF16) for source in (own, previous)])[None]
    return enc_grad, dec_grad


def chosen(inputs, targets, enc_w, enc_b, dec_w, dec_b):
    aligned = all(size % LANES == 0 for size in (*inputs.shape[1:], enc_w.shape[1]))
    fits = lax.axis_size("feat") == COUNT and dec_w.shape[1] == 2
    body = on_device if aligned and fits else plain
    return body(inputs, targets, enc_w, enc_b, dec_w, dec_b)


def solution(mesh):
    return jax.shard_map(
        chosen,
        mesh=mesh,
        in_specs=(
            P("section", None, "feat"),
            P("section", None, "feat"),
            P("section", "feat", None),
            P("section", "feat"),
            P("section", None, "feat", None),
            P("section", "feat"),
        ),
        out_specs=(P("section", "feat", None), P("section", None, "feat", None)),
        check_vma=False,
    )
```

```python
import functools

import jax
import jax.numpy as jnp
from jax import lax
from jax.experimental import pallas as pl
from jax.experimental.pallas import tpu as pltpu
from jax.sharding import PartitionSpec as P

LANES = 128
MIB = 1024 * 1024
BF16 = jnp.bfloat16
F32 = jnp.float32

SPLIT_FLOPS = 10**10

OFFSETS = (0, -1, 1, -2, 2, -3, 3, 4)
COUNT = len(OFFSETS)
NEAR = (0, 1, 2, 3)
FAR = (6, 4)
CROSSING = (7, 5)
BLOCKS = ((0, 1, 2, 3), (6, 4), (7, 5))


def from_behind(value, axis, steps):
    count = lax.axis_size(axis)
    initial, last = (max(0, -steps), min(count, count - steps))
    return lax.ppermute(value, axis, [(source, source + steps) for source in range(initial, last)])


def transposed(left, right):
    return lax.dot_general(left, right, (((0,), (0,)), ((), ())), preferred_element_type=F32)


def against(left, right):
    return lax.dot_general(left, right, (((1,), (1,)), ((), ())), preferred_element_type=F32)


def exchanged(value, mask):
    count = lax.axis_size("feat")
    return lax.ppermute(value, "feat", [(i, i ^ mask) for i in range(count)])


def ring(count):
    return [*range(0, count, 2), *range(count - 1, 0, -2)]


def passed_on(value, by):
    count = lax.axis_size("feat")
    order = ring(count)
    return lax.ppermute(value, "feat", [(order[p], order[(p + by) % count]) for p in range(count)])


def ring_owner(offset):
    count = COUNT
    me = lax.axis_index("feat")
    half = me // 2
    place = jnp.where(lax.rem(me, 2) == 0, half, count - 1 - half)
    place = lax.rem(place + offset + count, count)
    return jnp.where(place < count // 2, 2 * place, 2 * (count - 1 - place) + 1)


def split_kernel(in_ref, first_ref, last_ref):
    middle = first_ref.shape[0]
    first_ref[...] = in_ref[:middle, :]
    last_ref[...] = in_ref[middle:, :]


def ring_gather(own):
    count = lax.axis_size("feat")
    part = jax.ShapeDtypeStruct((own.shape[0] // 2, own.shape[1]), own.dtype)
    first, last = (
        {0: part}
        for part in pl.pallas_call(
            split_kernel,
            name="split",
            out_shape=(part, part),
            in_specs=vmem(1),
            out_specs=tuple(vmem(2)),
            compiler_params=params(2),
            cost_estimate=cost(SPLIT_FLOPS, 0),
        )(own)
    )
    for step in range(1, count // 2):
        for held in (first, last):
            held[-step] = passed_on(held[1 - step], 1)
            held[step] = passed_on(held[step - 1], -1)
    far = count // 2
    first[far] = passed_on(first[1 - far], 1)
    last[far] = passed_on(last[far - 1], -1)
    return first, last


def owner(mask):
    return jnp.bitwise_xor(lax.axis_index("feat"), mask)


def columns(index, width):
    return pl.ds(pl.multiple_of(index * width, width), width)


def vmem(count):
    return [pl.BlockSpec(memory_space=pltpu.VMEM)] * count


def params(mib):
    return pltpu.CompilerParams(vmem_limit_bytes=mib * MIB)


def flat(groups):
    return [(i, row, mask) for i, masks in enumerate(groups) for row, mask in enumerate(masks)]


def pack_kernel(*refs):
    out_ref, start = refs[-1], 0
    for ref in refs[:-1]:
        out_ref[start : start + ref.shape[0], :] = ref[...]
        start += ref.shape[0]


def packed(*parts):
    rows = sum(part.shape[0] for part in parts)
    return pl.pallas_call(
        pack_kernel,
        name="pack",
        out_shape=jax.ShapeDtypeStruct((rows, parts[0].shape[1]), parts[0].dtype),
        in_specs=vmem(len(parts)),
        out_specs=vmem(1)[0],
        compiler_params=params(1),
        cost_estimate=pl.CostEstimate(
            flops=0, bytes_accessed=4 * rows * parts[0].shape[1], transcendentals=0
        ),
    )(*parts)


def block(parts, k):
    return jnp.concatenate([parts[2 * k][...], parts[2 * k + 1][...]], axis=0)


def pre_kernel(*refs):
    count = len(OFFSETS)
    parts, (w_ref, b_ref, codes_ref, active_ref) = refs[: 2 * count], refs[2 * count :]
    width = parts[0].shape[1]
    steps, tile = tiles(w_ref.shape[0])
    for j in range(steps):
        here = slice(j * tile, (j + 1) * tile)
        total = None
        for k, offset in enumerate(OFFSETS):
            term = against(w_ref[here, columns(ring_owner(offset), width)], block(parts, k))
            total = term if total is None else total + term
        active = jnp.maximum(total.T + b_ref[:, here], 0.0)
        active_ref[:, here] = active
        codes_ref[:, here] = (active * active).astype(BF16)


def decoded(w_ref, slot, here, parts, groups, tok, total):
    width = parts[0].shape[1]
    for i, row, mask in flat(groups):
        part = parts[i][row * tok : (row + 1) * tok, :]
        term = against(w_ref[slot, here, columns(owner(mask), width)], part)
        total = term if total is None else total + term
    return total


def tiles(size):
    tile = 256 if size % 256 == 0 else LANES
    return size // tile, tile


def own_recon_kernel(*refs):
    parts, (w_ref, total_ref) = refs[: len(BLOCKS)], refs[len(BLOCKS) :]
    tok = total_ref.shape[1]
    steps, tile = tiles(w_ref.shape[1])

    for j in range(steps):
        here = slice(j * tile, (j + 1) * tile)
        total_ref[here, :] = decoded(w_ref, 0, here, parts, BLOCKS, tok, None)


def near_recon_kernel(part_ref, before_ref, w_ref, total_ref):
    tok = total_ref.shape[1]
    steps, tile = tiles(w_ref.shape[1])
    for j in range(steps):
        here = slice(j * tile, (j + 1) * tile)
        total_ref[here, :] = decoded(w_ref, 1, here, [part_ref], BLOCKS[:1], tok, before_ref[here, :])


def products(error_ref, w_ref, slot, masks, out_ref):
    tok = error_ref.shape[0]
    for row, mask in enumerate(masks):
        term = jnp.dot(
            error_ref[...], w_ref[slot, :, columns(owner(mask), out_ref.shape[1])], preferred_element_type=F32
        )
        out_ref[row * tok : (row + 1) * tok, :] = term.astype(out_ref.dtype)


def recon_kernel(scale, *refs):
    rest = BLOCKS[1:]
    parts, (total_ref, w_ref, b_ref, target_ref, error_ref, far_ref) = refs[: len(rest)], refs[len(rest) :]
    tok = total_ref.shape[1]
    steps, tile = tiles(w_ref.shape[1])

    for j in range(steps):
        here = slice(j * tile, (j + 1) * tile)
        total = decoded(w_ref, 1, here, parts, rest, tok, total_ref[here, :])
        error = total.T + b_ref[:, here] - target_ref[:, here].astype(F32)
        error_ref[:, here] = (error * scale).astype(BF16)

    products(error_ref, w_ref, 1, FAR + CROSSING, far_ref)


def own_grad_kernel(error_ref, w_ref, sent_ref, near_ref, far_ref):
    products(error_ref, w_ref, 1, NEAR, sent_ref)
    products(error_ref, w_ref, 0, FAR + CROSSING, far_ref)
    products(error_ref, w_ref, 0, NEAR, near_ref)


def written(blocks, left_ref, width, target, held, sems):
    steps, tile = tiles(left_ref.shape[0])
    copies = []
    for k, (value, index) in enumerate(blocks):
        buffer = held.at[k % 2]
        if k >= 2:
            copies[k - 2].wait()
        for j in range(steps):
            here = slice(j * tile, (j + 1) * tile)
            buffer[here, :] = jnp.dot(left_ref[here, :], value, preferred_element_type=F32).astype(BF16)
        copies.append(pltpu.make_async_copy(buffer, target(columns(index, width)), sems.at[k % 2]))
        copies[k].start()
    for copy in copies[-2:]:
        copy.wait()


def dec_grad_kernel(slot, held_count, *refs):
    error_ref, parts = refs[0], refs[1 : 1 + len(BLOCKS)]
    out_ref, left_ref, held, sems = refs[1 + len(BLOCKS) + held_count :]
    tok, width = error_ref.shape[0], parts[0].shape[1]
    left_ref[...] = error_ref[...].T
    blocks = [(parts[i][row * tok : (row + 1) * tok, :], owner(mask)) for i, row, mask in flat(BLOCKS)]
    written(blocks, left_ref, width, lambda here: out_ref.at[0, slot, :, here], held, sems)


def add_kernel(own_ref, arrived_ref, *outs):
    first = 0
    for out_ref in outs:
        here = slice(first, first + out_ref.shape[0])
        out_ref[...] = (own_ref[here, :] + arrived_ref[here, :].astype(F32)).astype(out_ref.dtype)
        first += out_ref.shape[0]


def enc_grad_kernel(*refs):
    grads, parts = refs[: -5 - 2 * COUNT], refs[-5 - 2 * COUNT : -5]
    active_ref, out_ref, left_ref, held, sems = refs[-5:]
    total = grads[0][...]
    for grad in grads[1:]:
        total = total + grad[...].astype(F32)
    left_ref[...] = (total * 2.0 * active_ref[...]).astype(BF16).T
    blocks = [(block(parts, k), ring_owner(offset)) for k, offset in enumerate(OFFSETS)]
    written(blocks, left_ref, parts[0].shape[1], lambda here: out_ref.at[0, :, here], held, sems)


def cost(flops, moved):
    return pl.CostEstimate(flops=flops, bytes_accessed=moved, transcendentals=0)


def on_device(inputs, targets, enc_w, enc_b, dec_w, dec_b):
    count = COUNT
    tok, width = inputs.shape[1:]
    own_features, model = enc_w.shape[1:]
    features = dec_w.shape[3]
    scale = tok ** (-0.5)
    matmul = 2 * tok * width * features
    struct = jax.ShapeDtypeStruct

    def stack(masks, kind):
        return struct((len(masks) * tok, own_features), kind)


    first, last = ring_gather(inputs[0])
    inputs_of = [part for offset in OFFSETS for part in (first[offset], last[offset])]
    enc_weights, weights = [pltpu.with_memory_space_constraint(w[0], pltpu.VMEM) for w in (enc_w, dec_w)]

    codes, active = pl.pallas_call(
        pre_kernel,
        name="pre",
        out_shape=(struct((tok, own_features), BF16), struct((tok, own_features), F32)),
        in_specs=vmem(2 * count + 2),
        out_specs=tuple(vmem(2)),
        compiler_params=params(16),
        cost_estimate=cost(2 * tok * own_features * model, 0),
    )(*inputs_of, enc_weights, enc_b)

    far_pair = packed(exchanged(codes, 6), exchanged(codes, 4))
    far_across = exchanged(far_pair, 1)
    own = [packed(codes, *[exchanged(codes, mask) for mask in (1, 2, 3)]), far_pair, far_across]
    previous = [from_behind(part, "section", 1) for part in own]

    total = pl.pallas_call(
        own_recon_kernel,
        name="own_recon",
        out_shape=struct((width, tok), F32),
        in_specs=vmem(len(own) + 1),
        out_specs=vmem(1)[0],
        compiler_params=params(8),
        cost_estimate=cost(matmul, 0),
    )(*own, weights)

    total = pl.pallas_call(
        near_recon_kernel,
        name="near_recon",
        out_shape=struct((width, tok), F32),
        in_specs=vmem(3),
        out_specs=vmem(1)[0],
        compiler_params=params(8),
        cost_estimate=cost(matmul // 2, 0),
    )(previous[0], total, weights)

    error, sent_far = pl.pallas_call(
        functools.partial(recon_kernel, scale),
        name="recon",
        out_shape=(struct((tok, width), BF16), stack(FAR + CROSSING, BF16)),
        in_specs=vmem(len(previous) + 3),
        out_specs=tuple(vmem(2)),
        compiler_params=params(8),
        cost_estimate=cost(2 * matmul, 4 * MIB),
    )(*previous[1:], total, weights, dec_b, targets[0])
    arrived_far = from_behind(sent_far, "section", -1)

    sent_near, own_near, own_far = pl.pallas_call(
        own_grad_kernel,
        name="own_grad",
        out_shape=(stack(NEAR, BF16), stack(NEAR, F32), stack(FAR + CROSSING, F32)),
        in_specs=vmem(2),
        out_specs=tuple(vmem(3)),
        compiler_params=params(8),
        cost_estimate=cost(3 * matmul // 2, 6 * MIB),
    )(error, weights)
    arrived_near = from_behind(sent_near, "section", -1)

    def buffers(rows, block_width):
        return [
            pltpu.VMEM((rows, tok), BF16),
            pltpu.VMEM((2, rows, block_width), BF16),
            pltpu.SemaphoreType.DMA((2,)),
        ]

    in_hbm = pl.BlockSpec(memory_space=pltpu.HBM)

    def dec_grad_slot(slot, parts, *held):
        return pl.pallas_call(
            functools.partial(dec_grad_kernel, slot, len(held)),
            name="dec_grad",
            out_shape=struct(dec_w.shape, BF16),
            in_specs=[*vmem(1 + len(parts)), *[in_hbm for _ in held]],
            out_specs=in_hbm,
            scratch_shapes=buffers(width, own_features),
            input_output_aliases={1 + len(parts): 0} if held else {},
            compiler_params=params(8),
            cost_estimate=cost(matmul, 2 * width * features),
        )(error, *parts, *held)

    dec_grad = dec_grad_slot(0, own)

    def sums(outs, own_part, arrived):
        return pl.pallas_call(
            add_kernel,
            name="sum",
            out_shape=tuple(stack(masks, kind) for masks, kind in outs),
            in_specs=vmem(2),
            out_specs=tuple(vmem(len(outs))),
            compiler_params=params(2),
            cost_estimate=cost(tok * features, 2 * MIB),
        )(own_part, arrived)

    kept, crossing = sums(((FAR, F32), (CROSSING, BF16)), own_far, arrived_far)
    lines = sums([((mask,), BF16) for mask in FAR], kept, exchanged(crossing, 1))
    near = sums([((mask,), BF16 if mask else F32) for mask in NEAR], own_near, arrived_near)
    grads = [
        near[0],
        *[exchanged(near[mask], mask) for mask in NEAR[1:]],
        *[exchanged(line, mask) for mask, line in zip(FAR, lines)],
    ]
    held_grad = pltpu.with_memory_space_constraint(dec_grad, pltpu.HBM)
    dec_grad = dec_grad_slot(1, previous, held_grad)

    enc_grad = pl.pallas_call(
        enc_grad_kernel,
        name="enc_grad",
        out_shape=struct(enc_w.shape, BF16),
        in_specs=vmem(len(grads) + 2 * count + 1),
        out_specs=in_hbm,
        scratch_shapes=buffers(own_features, width),
        compiler_params=params(8),
        cost_estimate=cost(matmul, 2 * own_features * model),
    )(*grads, *inputs_of, active)
    return enc_grad, dec_grad


def plain(inputs, targets, enc_w, enc_b, dec_w, dec_b):
    scale = inputs.shape[1] ** (-0.5)
    gathered = lax.all_gather(inputs[0], "feat", axis=1, tiled=True)
    active = jnp.maximum(against(gathered, enc_w[0]) + enc_b[0], 0.0)
    codes = (active * active).astype(BF16)
    own = lax.all_gather(codes, "feat", axis=1, tiled=True)
    previous = from_behind(own, "section", 1)
    weights = dec_w[0]
    total = dec_b[0] + against(own, weights[0]) + against(previous, weights[1])
    error = ((total - targets[0].astype(F32)) * scale).astype(BF16)
    sent = jnp.dot(error, weights[1], preferred_element_type=F32)
    code_grad = jnp.dot(error, weights[0], preferred_element_type=F32) + from_behind(sent, "section", -1)
    mine = lax.psum_scatter(code_grad, "feat", scatter_dimension=1, tiled=True)
    pre_grad = (mine * 2.0 * active).astype(BF16)
    enc_grad = transposed(pre_grad, gathered).astype(BF16)[None]
    dec_grad = jnp.stack([transposed(error, source).astype(BF16) for source in (own, previous)])[None]
    return enc_grad, dec_grad


def chosen(inputs, targets, enc_w, enc_b, dec_w, dec_b):
    aligned = all(size % LANES == 0 for size in (*inputs.shape[1:], enc_w.shape[1]))
    fits = lax.axis_size("feat") == COUNT and dec_w.shape[1] == 2
    body = on_device if aligned and fits else plain
    return body(inputs, targets, enc_w, enc_b, dec_w, dec_b)


def solution(mesh):
    return jax.shard_map(
        chosen,
        mesh=mesh,
        in_specs=(
            P("section", None, "feat"),
            P("section", None, "feat"),
            P("section", "feat", None),
            P("section", "feat"),
            P("section", None, "feat", None),
            P("section", "feat"),
        ),
        out_specs=(P("section", "feat", None), P("section", None, "feat", None)),
        check_vma=False,
    )
```

```python
import functools

import jax
import jax.numpy as jnp
from jax import lax
from jax.experimental import pallas as pl
from jax.experimental.pallas import tpu as pltpu
from jax.sharding import PartitionSpec as P

LANES = 128
MIB = 1024 * 1024
BF16 = jnp.bfloat16
F32 = jnp.float32

SPLIT_FLOPS = 10**10

OFFSETS = (0, -1, 1, -2, 2, -3, 3, 4)
COUNT = len(OFFSETS)
NEAR = (0, 1, 2, 3)
FAR = (6, 4)
CROSSING = (7, 5)
BLOCKS = ((0, 1, 2, 3), (6, 4), (7, 5))
EARLY = BLOCKS[:1]


def from_behind(value, axis, steps):
    count = lax.axis_size(axis)
    initial, last = (max(0, -steps), min(count, count - steps))
    return lax.ppermute(value, axis, [(source, source + steps) for source in range(initial, last)])


def diagonal(value):
    sections, count = lax.axis_size("section"), lax.axis_size("feat")
    pairs = [
        (s * count + i, (s + 1) * count + (i ^ 1)) for s in range(sections - 1) for i in range(count)
    ]
    return lax.ppermute(value, ("section", "feat"), pairs)


def transposed(left, right):
    return lax.dot_general(left, right, (((0,), (0,)), ((), ())), preferred_element_type=F32)


def against(left, right):
    return lax.dot_general(left, right, (((1,), (1,)), ((), ())), preferred_element_type=F32)


def exchanged(value, mask):
    count = lax.axis_size("feat")
    return lax.ppermute(value, "feat", [(i, i ^ mask) for i in range(count)])


def ring(count):
    return [*range(0, count, 2), *range(count - 1, 0, -2)]


def passed_on(value, by):
    count = lax.axis_size("feat")
    order = ring(count)
    return lax.ppermute(value, "feat", [(order[p], order[(p + by) % count]) for p in range(count)])


def ring_owner(offset):
    count = COUNT
    me = lax.axis_index("feat")
    half = me // 2
    place = jnp.where(lax.rem(me, 2) == 0, half, count - 1 - half)
    place = lax.rem(place + offset + count, count)
    return jnp.where(place < count // 2, 2 * place, 2 * (count - 1 - place) + 1)


def split_kernel(in_ref, first_ref, last_ref):
    middle = first_ref.shape[0]
    first_ref[...] = in_ref[:middle, :]
    last_ref[...] = in_ref[middle:, :]


def ring_gather(own):
    count = lax.axis_size("feat")
    part = jax.ShapeDtypeStruct((own.shape[0] // 2, own.shape[1]), own.dtype)
    first, last = (
        {0: part}
        for part in pl.pallas_call(
            split_kernel,
            name="split",
            out_shape=(part, part),
            in_specs=vmem(1),
            out_specs=tuple(vmem(2)),
            compiler_params=params(2),
            cost_estimate=cost(SPLIT_FLOPS, 0),
        )(own)
    )
    for step in range(1, count // 2):
        for held in (first, last):
            held[-step] = passed_on(held[1 - step], 1)
            held[step] = passed_on(held[step - 1], -1)
    far = count // 2
    first[far] = passed_on(first[1 - far], 1)
    last[far] = passed_on(last[far - 1], -1)
    return first, last


def owner(mask):
    return jnp.bitwise_xor(lax.axis_index("feat"), mask)


def columns(index, width):
    return pl.ds(pl.multiple_of(index * width, width), width)


def vmem(count):
    return [pl.BlockSpec(memory_space=pltpu.VMEM)] * count


def params(mib):
    return pltpu.CompilerParams(vmem_limit_bytes=mib * MIB)


def flat(groups):
    return [(i, row, mask) for i, masks in enumerate(groups) for row, mask in enumerate(masks)]


def pack_kernel(*refs):
    out_ref, start = refs[-1], 0
    for ref in refs[:-1]:
        out_ref[start : start + ref.shape[0], :] = ref[...]
        start += ref.shape[0]


def packed(*parts):
    rows = sum(part.shape[0] for part in parts)
    return pl.pallas_call(
        pack_kernel,
        name="pack",
        out_shape=jax.ShapeDtypeStruct((rows, parts[0].shape[1]), parts[0].dtype),
        in_specs=vmem(len(parts)),
        out_specs=vmem(1)[0],
        compiler_params=params(1),
        cost_estimate=pl.CostEstimate(
            flops=0, bytes_accessed=4 * rows * parts[0].shape[1], transcendentals=0
        ),
    )(*parts)


def block(parts, k):
    return jnp.concatenate([parts[2 * k][...], parts[2 * k + 1][...]], axis=0)


def pre_kernel(*refs):
    count = len(OFFSETS)
    parts, (w_ref, b_ref, codes_ref, active_ref) = refs[: 2 * count], refs[2 * count :]
    width = parts[0].shape[1]
    steps, tile = tiles(w_ref.shape[0])
    for j in range(steps):
        here = slice(j * tile, (j + 1) * tile)
        total = None
        for k, offset in enumerate(OFFSETS):
            term = against(w_ref[here, columns(ring_owner(offset), width)], block(parts, k))
            total = term if total is None else total + term
        active = jnp.maximum(total.T + b_ref[:, here], 0.0)
        active_ref[:, here] = active
        codes_ref[:, here] = (active * active).astype(BF16)


def decoded(w_ref, slot, here, parts, groups, tok, total):
    width = parts[0].shape[1]
    for i, row, mask in flat(groups):
        part = parts[i][row * tok : (row + 1) * tok, :]
        term = against(w_ref[slot, here, columns(owner(mask), width)], part)
        total = term if total is None else total + term
    return total


def tiles(size):
    tile = 256 if size % 256 == 0 else LANES
    return size // tile, tile


def own_recon_kernel(*refs):
    parts, (w_ref, total_ref) = refs[: len(BLOCKS)], refs[len(BLOCKS) :]
    tok = total_ref.shape[1]
    steps, tile = tiles(w_ref.shape[1])

    for j in range(steps):
        here = slice(j * tile, (j + 1) * tile)
        total_ref[here, :] = decoded(w_ref, 0, here, parts, BLOCKS, tok, None)


def near_recon_kernel(*refs):
    parts, (before_ref, w_ref, total_ref) = refs[: len(EARLY)], refs[len(EARLY) :]
    tok = total_ref.shape[1]
    steps, tile = tiles(w_ref.shape[1])
    for j in range(steps):
        here = slice(j * tile, (j + 1) * tile)
        total_ref[here, :] = decoded(w_ref, 1, here, parts, EARLY, tok, before_ref[here, :])


def products(error_ref, w_ref, slot, masks, out_ref):
    tok = error_ref.shape[0]
    for row, mask in enumerate(masks):
        term = jnp.dot(
            error_ref[...], w_ref[slot, :, columns(owner(mask), out_ref.shape[1])], preferred_element_type=F32
        )
        out_ref[row * tok : (row + 1) * tok, :] = term.astype(out_ref.dtype)


def recon_kernel(scale, *refs):
    rest = BLOCKS[len(EARLY) :]
    parts, (total_ref, w_ref, b_ref, target_ref, error_ref, far_ref) = refs[: len(rest)], refs[len(rest) :]
    tok = total_ref.shape[1]
    steps, tile = tiles(w_ref.shape[1])

    for j in range(steps):
        here = slice(j * tile, (j + 1) * tile)
        total = decoded(w_ref, 1, here, parts, rest, tok, total_ref[here, :])
        error = total.T + b_ref[:, here] - target_ref[:, here].astype(F32)
        error_ref[:, here] = (error * scale).astype(BF16)

    products(error_ref, w_ref, 1, FAR + CROSSING, far_ref)


def own_grad_kernel(error_ref, w_ref, sent_ref, near_ref, far_ref):
    products(error_ref, w_ref, 1, NEAR, sent_ref)
    products(error_ref, w_ref, 0, FAR + CROSSING, far_ref)
    products(error_ref, w_ref, 0, NEAR, near_ref)


def dec_grad_kernel(groups, *refs):
    error_ref, parts, out_ref = refs[0], refs[1 : 1 + len(groups)], refs[-1]
    width = parts[0].shape[1]
    tok = error_ref.shape[0]
    for i, row, mask in flat(groups):
        part = parts[i][row * tok : (row + 1) * tok, :]
        out_ref[0, 0, :, columns(owner(mask), width)] = transposed(error_ref[...], part).astype(BF16)


def add_kernel(own_ref, arrived_ref, *outs):
    first = 0
    for out_ref in outs:
        here = slice(first, first + out_ref.shape[0])
        out_ref[...] = (own_ref[here, :] + arrived_ref[here, :].astype(F32)).astype(out_ref.dtype)
        first += out_ref.shape[0]


def enc_grad_kernel(*refs):
    grads, parts = refs[: -2 - 2 * COUNT], refs[-2 - 2 * COUNT : -2]
    active_ref, out_ref = refs[-2:]
    width = parts[0].shape[1]
    total = grads[0][...]
    for grad in grads[1:]:
        total = total + grad[...].astype(F32)
    pre_grad = (total * 2.0 * active_ref[...]).astype(BF16)
    for k, offset in enumerate(OFFSETS):
        out_ref[0, :, columns(ring_owner(offset), width)] = transposed(pre_grad, block(parts, k)).astype(BF16)


def cost(flops, moved):
    return pl.CostEstimate(flops=flops, bytes_accessed=moved, transcendentals=0)


def on_device(inputs, targets, enc_w, enc_b, dec_w, dec_b):
    count = COUNT
    tok, width = inputs.shape[1:]
    own_features, model = enc_w.shape[1:]
    features = dec_w.shape[3]
    scale = tok ** (-0.5)
    matmul = 2 * tok * width * features
    struct = jax.ShapeDtypeStruct

    def stack(masks, kind):
        return struct((len(masks) * tok, own_features), kind)


    first, last = ring_gather(inputs[0])
    inputs_of = [part for offset in OFFSETS for part in (first[offset], last[offset])]
    enc_weights, weights = [pltpu.with_memory_space_constraint(w[0], pltpu.VMEM) for w in (enc_w, dec_w)]

    codes, active = pl.pallas_call(
        pre_kernel,
        name="pre",
        out_shape=(struct((tok, own_features), BF16), struct((tok, own_features), F32)),
        in_specs=vmem(2 * count + 2),
        out_specs=tuple(vmem(2)),
        compiler_params=params(16),
        cost_estimate=cost(2 * tok * own_features * model, 0),
    )(*inputs_of, enc_weights, enc_b)

    far_pair = packed(exchanged(codes, 6), exchanged(codes, 4))
    own = [packed(codes, *[exchanged(codes, mask) for mask in (1, 2, 3)]), far_pair, exchanged(far_pair, 1)]
    previous = [from_behind(part, "section", 1) for part in own[:2]]
    previous.append(diagonal(far_pair))

    total = pl.pallas_call(
        own_recon_kernel,
        name="own_recon",
        out_shape=struct((width, tok), F32),
        in_specs=vmem(len(own) + 1),
        out_specs=vmem(1)[0],
        compiler_params=params(8),
        cost_estimate=cost(matmul, 0),
    )(*own, weights)

    total = pl.pallas_call(
        near_recon_kernel,
        name="near_recon",
        out_shape=struct((width, tok), F32),
        in_specs=vmem(len(EARLY) + 2),
        out_specs=vmem(1)[0],
        compiler_params=params(8),
        cost_estimate=cost(matmul // 2, 0),
    )(*previous[: len(EARLY)], total, weights)

    error, sent_far = pl.pallas_call(
        functools.partial(recon_kernel, scale),
        name="recon",
        out_shape=(struct((tok, width), BF16), stack(FAR + CROSSING, BF16)),
        in_specs=vmem(len(previous) - len(EARLY) + 4),
        out_specs=tuple(vmem(2)),
        compiler_params=params(8),
        cost_estimate=cost(2 * matmul, 4 * MIB),
    )(*previous[len(EARLY) :], total, weights, dec_b, targets[0])
    arrived_far = from_behind(sent_far, "section", -1)

    sent_near, own_near, own_far = pl.pallas_call(
        own_grad_kernel,
        name="own_grad",
        out_shape=(stack(NEAR, BF16), stack(NEAR, F32), stack(FAR + CROSSING, F32)),
        in_specs=vmem(2),
        out_specs=tuple(vmem(3)),
        compiler_params=params(8),
        cost_estimate=cost(3 * matmul // 2, 6 * MIB),
    )(error, weights)
    arrived_near = from_behind(sent_near, "section", -1)

    rows = LANES

    def dec_grad_slot(slot, groups, parts, *held):
        return pl.pallas_call(
            functools.partial(dec_grad_kernel, groups),
            name="dec_grad",
            grid=(width // rows,),
            out_shape=struct(dec_w.shape, BF16),
            in_specs=[
                pl.BlockSpec((tok, rows), lambda j: (0, j)),
                *[pl.BlockSpec(part.shape, lambda j: (0, 0)) for part in parts],
                *[pl.BlockSpec(memory_space=pltpu.HBM) for _ in held],
            ],
            out_specs=pl.BlockSpec((1, 1, rows, features), lambda j: (0, slot, j, 0)),
            input_output_aliases={1 + len(parts): 0} if held else {},
            compiler_params=params(12),
            cost_estimate=cost(matmul, 2 * width * features),
        )(error, *parts, *held)

    dec_grad = dec_grad_slot(0, BLOCKS, own)

    def sums(outs, own_part, arrived):
        return pl.pallas_call(
            add_kernel,
            name="sum",
            out_shape=tuple(stack(masks, kind) for masks, kind in outs),
            in_specs=vmem(2),
            out_specs=tuple(vmem(len(outs))),
            compiler_params=params(2),
            cost_estimate=cost(tok * features, 2 * MIB),
        )(own_part, arrived)

    kept, crossing = sums(((FAR, F32), (CROSSING, BF16)), own_far, arrived_far)
    lines = sums([((mask,), BF16) for mask in FAR], kept, exchanged(crossing, 1))
    near = sums([((mask,), BF16 if mask else F32) for mask in NEAR], own_near, arrived_near)
    grads = [
        near[0],
        *[exchanged(near[mask], mask) for mask in NEAR[1:]],
        *[exchanged(line, mask) for mask, line in zip(FAR, lines)],
    ]
    held_grad = pltpu.with_memory_space_constraint(dec_grad, pltpu.HBM)
    dec_grad = dec_grad_slot(1, BLOCKS, previous, held_grad)

    enc_grad = pl.pallas_call(
        enc_grad_kernel,
        name="enc_grad",
        grid=(own_features // LANES,),
        out_shape=struct(enc_w.shape, BF16),
        in_specs=[
            *[pl.BlockSpec((tok, LANES), lambda j: (0, j))] * len(grads),
            *[pl.BlockSpec((tok // 2, width), lambda j: (0, 0))] * (2 * count),
            pl.BlockSpec((tok, LANES), lambda j: (0, j)),
        ],
        out_specs=pl.BlockSpec((1, LANES, model), lambda j: (0, j, 0)),
        compiler_params=params(16),
        cost_estimate=cost(matmul, 2 * own_features * model),
    )(*grads, *inputs_of, active)
    return enc_grad, dec_grad


def plain(inputs, targets, enc_w, enc_b, dec_w, dec_b):
    scale = inputs.shape[1] ** (-0.5)
    gathered = lax.all_gather(inputs[0], "feat", axis=1, tiled=True)
    active = jnp.maximum(against(gathered, enc_w[0]) + enc_b[0], 0.0)
    codes = (active * active).astype(BF16)
    own = lax.all_gather(codes, "feat", axis=1, tiled=True)
    previous = from_behind(own, "section", 1)
    weights = dec_w[0]
    total = dec_b[0] + against(own, weights[0]) + against(previous, weights[1])
    error = ((total - targets[0].astype(F32)) * scale).astype(BF16)
    sent = jnp.dot(error, weights[1], preferred_element_type=F32)
    code_grad = jnp.dot(error, weights[0], preferred_element_type=F32) + from_behind(sent, "section", -1)
    mine = lax.psum_scatter(code_grad, "feat", scatter_dimension=1, tiled=True)
    pre_grad = (mine * 2.0 * active).astype(BF16)
    enc_grad = transposed(pre_grad, gathered).astype(BF16)[None]
    dec_grad = jnp.stack([transposed(error, source).astype(BF16) for source in (own, previous)])[None]
    return enc_grad, dec_grad


def chosen(inputs, targets, enc_w, enc_b, dec_w, dec_b):
    aligned = all(size % LANES == 0 for size in (*inputs.shape[1:], enc_w.shape[1]))
    fits = lax.axis_size("feat") == COUNT and dec_w.shape[1] == 2
    body = on_device if aligned and fits else plain
    return body(inputs, targets, enc_w, enc_b, dec_w, dec_b)


def solution(mesh):
    return jax.shard_map(
        chosen,
        mesh=mesh,
        in_specs=(
            P("section", None, "feat"),
            P("section", None, "feat"),
            P("section", "feat", None),
            P("section", "feat"),
            P("section", None, "feat", None),
            P("section", "feat"),
        ),
        out_specs=(P("section", "feat", None), P("section", None, "feat", None)),
        check_vma=False,
    )
```

```python
import functools

import jax
import jax.numpy as jnp
from jax import lax
from jax.experimental import pallas as pl
from jax.experimental.pallas import tpu as pltpu
from jax.sharding import PartitionSpec as P

LANES = 128
MIB = 1024 * 1024
BF16 = jnp.bfloat16
F32 = jnp.float32

SPLIT_FLOPS = 10**10

OFFSETS = (0, -1, 1, -2, 2, -3, 3, 4)
COUNT = len(OFFSETS)
NEAR = (0, 1, 2, 3)
FAR = (6, 4)
CROSSING = (7, 5)
BLOCKS = ((0, 1, 2, 3), (6, 4), (7, 5))


def from_behind(value, axis, steps):
    count = lax.axis_size(axis)
    initial, last = (max(0, -steps), min(count, count - steps))
    return lax.ppermute(value, axis, [(source, source + steps) for source in range(initial, last)])


def transposed(left, right):
    return lax.dot_general(left, right, (((0,), (0,)), ((), ())), preferred_element_type=F32)


def against(left, right):
    return lax.dot_general(left, right, (((1,), (1,)), ((), ())), preferred_element_type=F32)


def exchanged(value, mask):
    count = lax.axis_size("feat")
    return lax.ppermute(value, "feat", [(i, i ^ mask) for i in range(count)])


def ring(count):
    return [*range(0, count, 2), *range(count - 1, 0, -2)]


def passed_on(value, by):
    count = lax.axis_size("feat")
    order = ring(count)
    return lax.ppermute(value, "feat", [(order[p], order[(p + by) % count]) for p in range(count)])


def ring_owner(offset):
    count = COUNT
    me = lax.axis_index("feat")
    half = me // 2
    place = jnp.where(lax.rem(me, 2) == 0, half, count - 1 - half)
    place = lax.rem(place + offset + count, count)
    return jnp.where(place < count // 2, 2 * place, 2 * (count - 1 - place) + 1)


def split_kernel(in_ref, first_ref, last_ref):
    middle = first_ref.shape[0]
    first_ref[...] = in_ref[:middle, :]
    last_ref[...] = in_ref[middle:, :]


def ring_gather(own):
    count = lax.axis_size("feat")
    part = jax.ShapeDtypeStruct((own.shape[0] // 2, own.shape[1]), own.dtype)
    first, last = (
        {0: part}
        for part in pl.pallas_call(
            split_kernel,
            name="split",
            out_shape=(part, part),
            in_specs=vmem(1),
            out_specs=tuple(vmem(2)),
            compiler_params=params(2),
            cost_estimate=cost(SPLIT_FLOPS, 0),
        )(own)
    )
    for step in range(1, count // 2):
        for held in (first, last):
            held[-step] = passed_on(held[1 - step], 1)
            held[step] = passed_on(held[step - 1], -1)
    far = count // 2
    first[far] = passed_on(first[1 - far], 1)
    last[far] = passed_on(last[far - 1], -1)
    return first, last


def owner(mask):
    return jnp.bitwise_xor(lax.axis_index("feat"), mask)


def columns(index, width):
    return pl.ds(pl.multiple_of(index * width, width), width)


def vmem(count):
    return [pl.BlockSpec(memory_space=pltpu.VMEM)] * count


def params(mib):
    return pltpu.CompilerParams(vmem_limit_bytes=mib * MIB)


def flat(groups):
    return [(i, row, mask) for i, masks in enumerate(groups) for row, mask in enumerate(masks)]


def pack_kernel(*refs):
    out_ref, start = refs[-1], 0
    for ref in refs[:-1]:
        out_ref[start : start + ref.shape[0], :] = ref[...]
        start += ref.shape[0]


def packed(*parts):
    rows = sum(part.shape[0] for part in parts)
    return pl.pallas_call(
        pack_kernel,
        name="pack",
        out_shape=jax.ShapeDtypeStruct((rows, parts[0].shape[1]), parts[0].dtype),
        in_specs=vmem(len(parts)),
        out_specs=vmem(1)[0],
        compiler_params=params(1),
        cost_estimate=pl.CostEstimate(
            flops=0, bytes_accessed=4 * rows * parts[0].shape[1], transcendentals=0
        ),
    )(*parts)


def block(parts, k):
    return jnp.concatenate([parts[2 * k][...], parts[2 * k + 1][...]], axis=0)


def pre_kernel(*refs):
    count = len(OFFSETS)
    parts, (w_ref, b_ref, codes_ref, active_ref) = refs[: 2 * count], refs[2 * count :]
    width = parts[0].shape[1]
    steps, tile = tiles(w_ref.shape[0])
    for j in range(steps):
        here = slice(j * tile, (j + 1) * tile)
        total = None
        for k, offset in enumerate(OFFSETS):
            term = against(w_ref[here, columns(ring_owner(offset), width)], block(parts, k))
            total = term if total is None else total + term
        active = jnp.maximum(total.T + b_ref[:, here], 0.0)
        active_ref[:, here] = active
        codes_ref[:, here] = (active * active).astype(BF16)


def decoded(w_ref, slot, here, parts, groups, tok, total):
    width = parts[0].shape[1]
    for i, row, mask in flat(groups):
        part = parts[i][row * tok : (row + 1) * tok, :]
        term = against(w_ref[slot, here, columns(owner(mask), width)], part)
        total = term if total is None else total + term
    return total


def tiles(size):
    tile = 256 if size % 256 == 0 else LANES
    return size // tile, tile


def own_recon_kernel(*refs):
    parts, (w_ref, total_ref) = refs[: len(BLOCKS)], refs[len(BLOCKS) :]
    tok = total_ref.shape[1]
    steps, tile = tiles(w_ref.shape[1])

    for j in range(steps):
        here = slice(j * tile, (j + 1) * tile)
        total_ref[here, :] = decoded(w_ref, 0, here, parts, BLOCKS, tok, None)


def near_recon_kernel(part_ref, before_ref, w_ref, total_ref):
    tok = total_ref.shape[1]
    steps, tile = tiles(w_ref.shape[1])
    for j in range(steps):
        here = slice(j * tile, (j + 1) * tile)
        total_ref[here, :] = decoded(w_ref, 1, here, [part_ref], BLOCKS[:1], tok, before_ref[here, :])


def products(error_ref, w_ref, slot, masks, out_ref):
    tok = error_ref.shape[0]
    for row, mask in enumerate(masks):
        term = jnp.dot(
            error_ref[...], w_ref[slot, :, columns(owner(mask), out_ref.shape[1])], preferred_element_type=F32
        )
        out_ref[row * tok : (row + 1) * tok, :] = term.astype(out_ref.dtype)


def recon_kernel(scale, *refs):
    rest = BLOCKS[1:]
    parts, (total_ref, w_ref, b_ref, target_ref, error_ref, far_ref) = refs[: len(rest)], refs[len(rest) :]
    tok = total_ref.shape[1]
    steps, tile = tiles(w_ref.shape[1])

    for j in range(steps):
        here = slice(j * tile, (j + 1) * tile)
        total = decoded(w_ref, 1, here, parts, rest, tok, total_ref[here, :])
        error = total.T + b_ref[:, here] - target_ref[:, here].astype(F32)
        error_ref[:, here] = (error * scale).astype(BF16)

    products(error_ref, w_ref, 1, FAR + CROSSING, far_ref)


def own_grad_kernel(error_ref, w_ref, sent_ref, near_ref, far_ref):
    products(error_ref, w_ref, 1, NEAR, sent_ref)
    products(error_ref, w_ref, 0, FAR + CROSSING, far_ref)
    products(error_ref, w_ref, 0, NEAR, near_ref)


def dec_grad_kernel(groups, *refs):
    error_ref, parts, out_ref = refs[0], refs[1 : 1 + len(groups)], refs[-1]
    width = parts[0].shape[1]
    tok = error_ref.shape[0]
    for i, row, mask in flat(groups):
        part = parts[i][row * tok : (row + 1) * tok, :]
        out_ref[0, 0, :, columns(owner(mask), width)] = transposed(error_ref[...], part).astype(BF16)


def add_kernel(own_ref, arrived_ref, *outs):
    first = 0
    for out_ref in outs:
        here = slice(first, first + out_ref.shape[0])
        out_ref[...] = (own_ref[here, :] + arrived_ref[here, :].astype(F32)).astype(out_ref.dtype)
        first += out_ref.shape[0]


def enc_grad_kernel(*refs):
    grads, parts = refs[: -2 - 2 * COUNT], refs[-2 - 2 * COUNT : -2]
    active_ref, out_ref = refs[-2:]
    width = parts[0].shape[1]
    total = grads[0][...]
    for grad in grads[1:]:
        total = total + grad[...].astype(F32)
    pre_grad = (total * 2.0 * active_ref[...]).astype(BF16)
    for k, offset in enumerate(OFFSETS):
        out_ref[0, :, columns(ring_owner(offset), width)] = transposed(pre_grad, block(parts, k)).astype(BF16)


def cost(flops, moved):
    return pl.CostEstimate(flops=flops, bytes_accessed=moved, transcendentals=0)


def on_device(inputs, targets, enc_w, enc_b, dec_w, dec_b):
    count = COUNT
    tok, width = inputs.shape[1:]
    own_features, model = enc_w.shape[1:]
    features = dec_w.shape[3]
    scale = tok ** (-0.5)
    matmul = 2 * tok * width * features
    struct = jax.ShapeDtypeStruct

    def stack(masks, kind):
        return struct((len(masks) * tok, own_features), kind)


    first, last = ring_gather(inputs[0])
    inputs_of = [part for offset in OFFSETS for part in (first[offset], last[offset])]
    enc_weights, weights = [pltpu.with_memory_space_constraint(w[0], pltpu.VMEM) for w in (enc_w, dec_w)]

    codes, active = pl.pallas_call(
        pre_kernel,
        name="pre",
        out_shape=(struct((tok, own_features), BF16), struct((tok, own_features), F32)),
        in_specs=vmem(2 * count + 2),
        out_specs=tuple(vmem(2)),
        compiler_params=params(16),
        cost_estimate=cost(2 * tok * own_features * model, 0),
    )(*inputs_of, enc_weights, enc_b)

    far_pair = packed(exchanged(codes, 6), exchanged(codes, 4))
    far_across = exchanged(far_pair, 1)
    own = [packed(codes, *[exchanged(codes, mask) for mask in (1, 2, 3)]), far_pair, far_across]
    previous = [from_behind(part, "section", 1) for part in own]

    total = pl.pallas_call(
        own_recon_kernel,
        name="own_recon",
        out_shape=struct((width, tok), F32),
        in_specs=vmem(len(own) + 1),
        out_specs=vmem(1)[0],
        compiler_params=params(8),
        cost_estimate=cost(matmul, 0),
    )(*own, weights)

    total = pl.pallas_call(
        near_recon_kernel,
        name="near_recon",
        out_shape=struct((width, tok), F32),
        in_specs=vmem(3),
        out_specs=vmem(1)[0],
        compiler_params=params(8),
        cost_estimate=cost(matmul // 2, 0),
    )(previous[0], total, weights)

    error, sent_far = pl.pallas_call(
        functools.partial(recon_kernel, scale),
        name="recon",
        out_shape=(struct((tok, width), BF16), stack(FAR + CROSSING, BF16)),
        in_specs=vmem(len(previous) + 3),
        out_specs=tuple(vmem(2)),
        compiler_params=params(8),
        cost_estimate=cost(2 * matmul, 4 * MIB),
    )(*previous[1:], total, weights, dec_b, targets[0])
    arrived_far = from_behind(sent_far, "section", -1)

    sent_near, own_near, own_far = pl.pallas_call(
        own_grad_kernel,
        name="own_grad",
        out_shape=(stack(NEAR, BF16), stack(NEAR, F32), stack(FAR + CROSSING, F32)),
        in_specs=vmem(2),
        out_specs=tuple(vmem(3)),
        compiler_params=params(8),
        cost_estimate=cost(3 * matmul // 2, 6 * MIB),
    )(error, weights)
    arrived_near = from_behind(sent_near, "section", -1)

    rows = 256 if width % 256 == 0 else LANES

    def dec_grad_slot(slot, groups, parts, *held):
        return pl.pallas_call(
            functools.partial(dec_grad_kernel, groups),
            name="dec_grad",
            grid=(width // rows,),
            out_shape=struct(dec_w.shape, BF16),
            in_specs=[
                pl.BlockSpec((tok, rows), lambda j: (0, j)),
                *[pl.BlockSpec(part.shape, lambda j: (0, 0)) for part in parts],
                *[pl.BlockSpec(memory_space=pltpu.HBM) for _ in held],
            ],
            out_specs=pl.BlockSpec((1, 1, rows, features), lambda j: (0, slot, j, 0)),
            input_output_aliases={1 + len(parts): 0} if held else {},
            compiler_params=params(12),
            cost_estimate=cost(matmul, 2 * width * features),
        )(error, *parts, *held)

    dec_grad = dec_grad_slot(0, BLOCKS, own)

    def sums(outs, own_part, arrived):
        return pl.pallas_call(
            add_kernel,
            name="sum",
            out_shape=tuple(stack(masks, kind) for masks, kind in outs),
            in_specs=vmem(2),
            out_specs=tuple(vmem(len(outs))),
            compiler_params=params(2),
            cost_estimate=cost(tok * features, 2 * MIB),
        )(own_part, arrived)

    kept, crossing = sums(((FAR, F32), (CROSSING, BF16)), own_far, arrived_far)
    lines = sums([((mask,), BF16) for mask in FAR], kept, exchanged(crossing, 1))
    near = sums([((mask,), BF16 if mask else F32) for mask in NEAR], own_near, arrived_near)
    grads = [
        near[0],
        *[exchanged(near[mask], mask) for mask in NEAR[1:]],
        *[exchanged(line, mask) for mask, line in zip(FAR, lines)],
    ]
    held_grad = pltpu.with_memory_space_constraint(dec_grad, pltpu.HBM)
    dec_grad = dec_grad_slot(1, BLOCKS, previous, held_grad)

    block_rows = tiles(own_features)[1]
    enc_grad = pl.pallas_call(
        enc_grad_kernel,
        name="enc_grad",
        grid=(own_features // block_rows,),
        out_shape=struct(enc_w.shape, BF16),
        in_specs=[
            *[pl.BlockSpec((tok, block_rows), lambda j: (0, j))] * len(grads),
            *[pl.BlockSpec((tok // 2, width), lambda j: (0, 0))] * (2 * count),
            pl.BlockSpec((tok, block_rows), lambda j: (0, j)),
        ],
        out_specs=pl.BlockSpec((1, block_rows, model), lambda j: (0, j, 0)),
        compiler_params=params(24),
        cost_estimate=cost(matmul, 2 * own_features * model),
    )(*grads, *inputs_of, active)
    return enc_grad, dec_grad


def plain(inputs, targets, enc_w, enc_b, dec_w, dec_b):
    scale = inputs.shape[1] ** (-0.5)
    gathered = lax.all_gather(inputs[0], "feat", axis=1, tiled=True)
    active = jnp.maximum(against(gathered, enc_w[0]) + enc_b[0], 0.0)
    codes = (active * active).astype(BF16)
    own = lax.all_gather(codes, "feat", axis=1, tiled=True)
    previous = from_behind(own, "section", 1)
    weights = dec_w[0]
    total = dec_b[0] + against(own, weights[0]) + against(previous, weights[1])
    error = ((total - targets[0].astype(F32)) * scale).astype(BF16)
    sent = jnp.dot(error, weights[1], preferred_element_type=F32)
    code_grad = jnp.dot(error, weights[0], preferred_element_type=F32) + from_behind(sent, "section", -1)
    mine = lax.psum_scatter(code_grad, "feat", scatter_dimension=1, tiled=True)
    pre_grad = (mine * 2.0 * active).astype(BF16)
    enc_grad = transposed(pre_grad, gathered).astype(BF16)[None]
    dec_grad = jnp.stack([transposed(error, source).astype(BF16) for source in (own, previous)])[None]
    return enc_grad, dec_grad


def chosen(inputs, targets, enc_w, enc_b, dec_w, dec_b):
    aligned = all(size % LANES == 0 for size in (*inputs.shape[1:], enc_w.shape[1]))
    fits = lax.axis_size("feat") == COUNT and dec_w.shape[1] == 2
    body = on_device if aligned and fits else plain
    return body(inputs, targets, enc_w, enc_b, dec_w, dec_b)


def solution(mesh):
    return jax.shard_map(
        chosen,
        mesh=mesh,
        in_specs=(
            P("section", None, "feat"),
            P("section", None, "feat"),
            P("section", "feat", None),
            P("section", "feat"),
            P("section", None, "feat", None),
            P("section", "feat"),
        ),
        out_specs=(P("section", "feat", None), P("section", None, "feat", None)),
        check_vma=False,
    )
```

```python
import functools

import jax
import jax.numpy as jnp
from jax import lax
from jax.experimental import pallas as pl
from jax.experimental.pallas import tpu as pltpu
from jax.sharding import PartitionSpec as P

LANES = 128
MIB = 1024 * 1024
BF16 = jnp.bfloat16
F32 = jnp.float32

SPLIT_FLOPS = 10**10

OFFSETS = (0, -1, 1, -2, 2, -3, 3, 4)
COUNT = len(OFFSETS)
NEAR = (0, 1, 2, 3)
FAR = (6, 4)
CROSSING = (7, 5)
BLOCKS = ((0, 1, 2, 3), (6, 4), (7, 5))


def from_behind(value, axis, steps):
    count = lax.axis_size(axis)
    initial, last = (max(0, -steps), min(count, count - steps))
    return lax.ppermute(value, axis, [(source, source + steps) for source in range(initial, last)])


def transposed(left, right):
    return lax.dot_general(left, right, (((0,), (0,)), ((), ())), preferred_element_type=F32)


def against(left, right):
    return lax.dot_general(left, right, (((1,), (1,)), ((), ())), preferred_element_type=F32)


def exchanged(value, mask):
    count = lax.axis_size("feat")
    return lax.ppermute(value, "feat", [(i, i ^ mask) for i in range(count)])


def ring(count):
    return [*range(0, count, 2), *range(count - 1, 0, -2)]


def passed_on(value, by):
    count = lax.axis_size("feat")
    order = ring(count)
    return lax.ppermute(value, "feat", [(order[p], order[(p + by) % count]) for p in range(count)])


def ring_owner(offset):
    count = COUNT
    me = lax.axis_index("feat")
    half = me // 2
    place = jnp.where(lax.rem(me, 2) == 0, half, count - 1 - half)
    place = lax.rem(place + offset + count, count)
    return jnp.where(place < count // 2, 2 * place, 2 * (count - 1 - place) + 1)


def split_kernel(in_ref, first_ref, last_ref):
    middle = first_ref.shape[0]
    first_ref[...] = in_ref[:middle, :]
    last_ref[...] = in_ref[middle:, :]


def ring_gather(own):
    count = lax.axis_size("feat")
    part = jax.ShapeDtypeStruct((own.shape[0] // 2, own.shape[1]), own.dtype)
    first, last = (
        {0: part}
        for part in pl.pallas_call(
            split_kernel,
            name="split",
            out_shape=(part, part),
            in_specs=vmem(1),
            out_specs=tuple(vmem(2)),
            compiler_params=params(2),
            cost_estimate=cost(SPLIT_FLOPS, 0),
        )(own)
    )
    for step in range(1, count // 2):
        for held in (first, last):
            held[-step] = passed_on(held[1 - step], 1)
            held[step] = passed_on(held[step - 1], -1)
    far = count // 2
    first[far] = passed_on(first[1 - far], 1)
    last[far] = passed_on(last[far - 1], -1)
    return first, last


def owner(mask):
    return jnp.bitwise_xor(lax.axis_index("feat"), mask)


def columns(index, width):
    return pl.ds(pl.multiple_of(index * width, width), width)


def vmem(count):
    return [pl.BlockSpec(memory_space=pltpu.VMEM)] * count


def params(mib):
    return pltpu.CompilerParams(vmem_limit_bytes=mib * MIB)


def flat(groups):
    return [(i, row, mask) for i, masks in enumerate(groups) for row, mask in enumerate(masks)]


def pack_kernel(*refs):
    out_ref, start = refs[-1], 0
    for ref in refs[:-1]:
        out_ref[start : start + ref.shape[0], :] = ref[...]
        start += ref.shape[0]


def packed(*parts):
    rows = sum(part.shape[0] for part in parts)
    return pl.pallas_call(
        pack_kernel,
        name="pack",
        out_shape=jax.ShapeDtypeStruct((rows, parts[0].shape[1]), parts[0].dtype),
        in_specs=vmem(len(parts)),
        out_specs=vmem(1)[0],
        compiler_params=params(1),
        cost_estimate=pl.CostEstimate(
            flops=0, bytes_accessed=4 * rows * parts[0].shape[1], transcendentals=0
        ),
    )(*parts)


def block(parts, k):
    return jnp.concatenate([parts[2 * k][...], parts[2 * k + 1][...]], axis=0)


def pre_kernel(*refs):
    count = len(OFFSETS)
    parts, (w_ref, b_ref, codes_ref, active_ref) = refs[: 2 * count], refs[2 * count :]
    width = parts[0].shape[1]
    steps, tile = tiles(w_ref.shape[0])
    for j in range(steps):
        here = slice(j * tile, (j + 1) * tile)
        total = None
        for k, offset in enumerate(OFFSETS):
            term = against(w_ref[here, columns(ring_owner(offset), width)], block(parts, k))
            total = term if total is None else total + term
        active = jnp.maximum(total.T + b_ref[:, here], 0.0)
        active_ref[:, here] = active
        codes_ref[:, here] = (active * active).astype(BF16)


def decoded(w_ref, slot, here, parts, groups, tok, total):
    width = parts[0].shape[1]
    for i, row, mask in flat(groups):
        part = parts[i][row * tok : (row + 1) * tok, :]
        term = against(w_ref[slot, here, columns(owner(mask), width)], part)
        total = term if total is None else total + term
    return total


def tiles(size):
    tile = 256 if size % 256 == 0 else LANES
    return size // tile, tile


def own_recon_kernel(*refs):
    parts, (w_ref, total_ref) = refs[: len(BLOCKS)], refs[len(BLOCKS) :]
    tok = total_ref.shape[1]
    steps, tile = tiles(w_ref.shape[1])

    for j in range(steps):
        here = slice(j * tile, (j + 1) * tile)
        total_ref[here, :] = decoded(w_ref, 0, here, parts, BLOCKS, tok, None)


def near_recon_kernel(part_ref, before_ref, w_ref, total_ref):
    tok = total_ref.shape[1]
    steps, tile = tiles(w_ref.shape[1])
    for j in range(steps):
        here = slice(j * tile, (j + 1) * tile)
        total_ref[here, :] = decoded(w_ref, 1, here, [part_ref], BLOCKS[:1], tok, before_ref[here, :])


def products(error_ref, w_ref, slot, masks, out_ref):
    tok = error_ref.shape[0]
    for row, mask in enumerate(masks):
        term = jnp.dot(
            error_ref[...], w_ref[slot, :, columns(owner(mask), out_ref.shape[1])], preferred_element_type=F32
        )
        out_ref[row * tok : (row + 1) * tok, :] = term.astype(out_ref.dtype)


def recon_kernel(scale, *refs):
    rest = BLOCKS[1:]
    parts, (total_ref, w_ref, b_ref, target_ref, error_ref, far_ref) = refs[: len(rest)], refs[len(rest) :]
    tok = total_ref.shape[1]
    steps, tile = tiles(w_ref.shape[1])

    for j in range(steps):
        here = slice(j * tile, (j + 1) * tile)
        total = decoded(w_ref, 1, here, parts, rest, tok, total_ref[here, :])
        error = total.T + b_ref[:, here] - target_ref[:, here].astype(F32)
        error_ref[:, here] = (error * scale).astype(BF16)

    products(error_ref, w_ref, 1, FAR + CROSSING, far_ref)


def own_grad_kernel(error_ref, w_ref, sent_ref, near_ref, far_ref):
    products(error_ref, w_ref, 1, NEAR, sent_ref)
    products(error_ref, w_ref, 0, FAR + CROSSING, far_ref)
    products(error_ref, w_ref, 0, NEAR, near_ref)


def dec_grad_kernel(groups, *refs):
    error_ref, parts, out_ref = refs[0], refs[1 : 1 + len(groups)], refs[-1]
    width = parts[0].shape[1]
    tok = error_ref.shape[0]
    for i, row, mask in flat(groups):
        part = parts[i][row * tok : (row + 1) * tok, :]
        out_ref[0, 0, :, columns(owner(mask), width)] = transposed(error_ref[...], part).astype(BF16)


def add_kernel(count, first, own_ref, arrived_ref, *refs):
    for out_ref in refs[-count:]:
        here = slice(first, first + out_ref.shape[0])
        out_ref[...] = (own_ref[here, :] + arrived_ref[here, :].astype(F32)).astype(out_ref.dtype)
        first += out_ref.shape[0]


def enc_grad_kernel(*refs):
    grads, parts = refs[: -2 - 2 * COUNT], refs[-2 - 2 * COUNT : -2]
    active_ref, out_ref = refs[-2:]
    width = parts[0].shape[1]
    total = grads[0][...]
    for grad in grads[1:]:
        total = total + grad[...].astype(F32)
    pre_grad = (total * 2.0 * active_ref[...]).astype(BF16)
    for k, offset in enumerate(OFFSETS):
        out_ref[0, :, columns(ring_owner(offset), width)] = transposed(pre_grad, block(parts, k)).astype(BF16)


def cost(flops, moved):
    return pl.CostEstimate(flops=flops, bytes_accessed=moved, transcendentals=0)


def on_device(inputs, targets, enc_w, enc_b, dec_w, dec_b):
    count = COUNT
    tok, width = inputs.shape[1:]
    own_features, model = enc_w.shape[1:]
    features = dec_w.shape[3]
    scale = tok ** (-0.5)
    matmul = 2 * tok * width * features
    struct = jax.ShapeDtypeStruct

    def stack(masks, kind):
        return struct((len(masks) * tok, own_features), kind)


    first, last = ring_gather(inputs[0])
    inputs_of = [part for offset in OFFSETS for part in (first[offset], last[offset])]
    enc_weights, weights = [pltpu.with_memory_space_constraint(w[0], pltpu.VMEM) for w in (enc_w, dec_w)]

    codes, active = pl.pallas_call(
        pre_kernel,
        name="pre",
        out_shape=(struct((tok, own_features), BF16), struct((tok, own_features), F32)),
        in_specs=vmem(2 * count + 2),
        out_specs=tuple(vmem(2)),
        compiler_params=params(16),
        cost_estimate=cost(2 * tok * own_features * model, 0),
    )(*inputs_of, enc_weights, enc_b)

    far_pair = packed(exchanged(codes, 6), exchanged(codes, 4))
    far_across = exchanged(far_pair, 1)
    own = [packed(codes, *[exchanged(codes, mask) for mask in (1, 2, 3)]), far_pair, far_across]
    previous = [from_behind(part, "section", 1) for part in own]

    total = pl.pallas_call(
        own_recon_kernel,
        name="own_recon",
        out_shape=struct((width, tok), F32),
        in_specs=vmem(len(own) + 1),
        out_specs=vmem(1)[0],
        compiler_params=params(8),
        cost_estimate=cost(matmul, 0),
    )(*own, weights)

    total = pl.pallas_call(
        near_recon_kernel,
        name="near_recon",
        out_shape=struct((width, tok), F32),
        in_specs=vmem(3),
        out_specs=vmem(1)[0],
        compiler_params=params(8),
        cost_estimate=cost(matmul // 2, 0),
    )(previous[0], total, weights)

    error, sent_far = pl.pallas_call(
        functools.partial(recon_kernel, scale),
        name="recon",
        out_shape=(struct((tok, width), BF16), stack(FAR + CROSSING, BF16)),
        in_specs=vmem(len(previous) + 3),
        out_specs=tuple(vmem(2)),
        compiler_params=params(8),
        cost_estimate=cost(2 * matmul, 4 * MIB),
    )(*previous[1:], total, weights, dec_b, targets[0])
    arrived_far = from_behind(sent_far, "section", -1)

    sent_near, own_near, own_far = pl.pallas_call(
        own_grad_kernel,
        name="own_grad",
        out_shape=(stack(NEAR, BF16), stack(NEAR, F32), stack(FAR + CROSSING, F32)),
        in_specs=vmem(2),
        out_specs=tuple(vmem(3)),
        compiler_params=params(8),
        cost_estimate=cost(3 * matmul // 2, 6 * MIB),
    )(error, weights)
    arrived_near = from_behind(sent_near, "section", -1)

    rows = 256 if width % 256 == 0 else LANES

    def sums(outs, own_part, arrived, *after, first=0):
        return pl.pallas_call(
            functools.partial(add_kernel, len(outs), first),
            name="sum",
            out_shape=tuple(stack(masks, kind) for masks, kind in outs),
            in_specs=[*vmem(2), *[pl.BlockSpec(memory_space=kind) for _, kind in after]],
            out_specs=tuple(vmem(len(outs))),
            compiler_params=params(2),
            cost_estimate=cost(tok * features, 2 * MIB),
        )(own_part, arrived, *[value for value, _ in after])

    def dec_grad_slot(slot, groups, parts, before, held):
        return pl.pallas_call(
            functools.partial(dec_grad_kernel, groups),
            name="dec_grad",
            grid=(width // rows,),
            out_shape=struct(dec_w.shape, BF16),
            in_specs=[
                pl.BlockSpec((tok, rows), lambda j: (0, j)),
                *[pl.BlockSpec(part.shape, lambda j: (0, 0)) for part in parts],
                pl.BlockSpec(memory_space=pltpu.HBM) if held else pl.BlockSpec(memory_space=pl.ANY),
            ],
            out_specs=pl.BlockSpec((1, 1, rows, features), lambda j: (0, slot, j, 0)),
            input_output_aliases={1 + len(parts): 0} if held else {},
            compiler_params=params(12),
            cost_estimate=cost(matmul, 2 * width * features),
        )(error, *parts, before)

    kept, crossing = sums(((FAR, F32), (CROSSING, BF16)), own_far, arrived_far)
    dec_grad = dec_grad_slot(0, BLOCKS, own, crossing, False)
    held_grad = pltpu.with_memory_space_constraint(dec_grad, pltpu.HBM)
    lines = sums(
        [((mask,), BF16) for mask in FAR], kept, exchanged(crossing, 1), (held_grad, pltpu.HBM)
    )
    mine, across = sums([((0,), F32), ((1,), BF16)], own_near, arrived_near, (lines[0], pltpu.VMEM))
    across = exchanged(across, 1)
    near = sums(
        [((2,), BF16), ((3,), BF16)], own_near, arrived_near, (across, pltpu.VMEM), first=2 * tok
    )
    grads = [
        mine,
        across,
        *[exchanged(line, mask) for mask, line in zip(FAR, lines)],
        *[exchanged(part, mask) for mask, part in zip((2, 3), near)],
    ]
    dec_grad = dec_grad_slot(1, BLOCKS, previous, held_grad, True)

    block_rows = tiles(own_features)[1]
    enc_grad = pl.pallas_call(
        enc_grad_kernel,
        name="enc_grad",
        grid=(own_features // block_rows,),
        out_shape=struct(enc_w.shape, BF16),
        in_specs=[
            *[pl.BlockSpec((tok, block_rows), lambda j: (0, j))] * len(grads),
            *[pl.BlockSpec((tok // 2, width), lambda j: (0, 0))] * (2 * count),
            pl.BlockSpec((tok, block_rows), lambda j: (0, j)),
        ],
        out_specs=pl.BlockSpec((1, block_rows, model), lambda j: (0, j, 0)),
        compiler_params=params(24),
        cost_estimate=cost(matmul, 2 * own_features * model),
    )(*grads, *inputs_of, active)
    return enc_grad, dec_grad


def plain(inputs, targets, enc_w, enc_b, dec_w, dec_b):
    scale = inputs.shape[1] ** (-0.5)
    gathered = lax.all_gather(inputs[0], "feat", axis=1, tiled=True)
    active = jnp.maximum(against(gathered, enc_w[0]) + enc_b[0], 0.0)
    codes = (active * active).astype(BF16)
    own = lax.all_gather(codes, "feat", axis=1, tiled=True)
    previous = from_behind(own, "section", 1)
    weights = dec_w[0]
    total = dec_b[0] + against(own, weights[0]) + against(previous, weights[1])
    error = ((total - targets[0].astype(F32)) * scale).astype(BF16)
    sent = jnp.dot(error, weights[1], preferred_element_type=F32)
    code_grad = jnp.dot(error, weights[0], preferred_element_type=F32) + from_behind(sent, "section", -1)
    mine = lax.psum_scatter(code_grad, "feat", scatter_dimension=1, tiled=True)
    pre_grad = (mine * 2.0 * active).astype(BF16)
    enc_grad = transposed(pre_grad, gathered).astype(BF16)[None]
    dec_grad = jnp.stack([transposed(error, source).astype(BF16) for source in (own, previous)])[None]
    return enc_grad, dec_grad


def chosen(inputs, targets, enc_w, enc_b, dec_w, dec_b):
    aligned = all(size % LANES == 0 for size in (*inputs.shape[1:], enc_w.shape[1]))
    fits = lax.axis_size("feat") == COUNT and dec_w.shape[1] == 2
    body = on_device if aligned and fits else plain
    return body(inputs, targets, enc_w, enc_b, dec_w, dec_b)


def solution(mesh):
    return jax.shard_map(
        chosen,
        mesh=mesh,
        in_specs=(
            P("section", None, "feat"),
            P("section", None, "feat"),
            P("section", "feat", None),
            P("section", "feat"),
            P("section", None, "feat", None),
            P("section", "feat"),
        ),
        out_specs=(P("section", "feat", None), P("section", None, "feat", None)),
        check_vma=False,
    )
```

```python
import functools

import jax
import jax.numpy as jnp
from jax import lax
from jax.experimental import pallas as pl
from jax.experimental.pallas import tpu as pltpu
from jax.sharding import PartitionSpec as P

LANES = 128
MIB = 1024 * 1024
BF16 = jnp.bfloat16
F32 = jnp.float32

SPLIT_FLOPS = 10**10

OFFSETS = (0, -1, 1, -2, 2, -3, 3, 4)
COUNT = len(OFFSETS)
NEAR = (0, 1, 2, 3)
FAR = (6, 4)
CROSSING = (7, 5)
BLOCKS = ((0, 1, 2, 3), (6, 4), (7, 5))


def from_behind(value, axis, steps):
    count = lax.axis_size(axis)
    initial, last = (max(0, -steps), min(count, count - steps))
    return lax.ppermute(value, axis, [(source, source + steps) for source in range(initial, last)])


def transposed(left, right):
    return lax.dot_general(left, right, (((0,), (0,)), ((), ())), preferred_element_type=F32)


def against(left, right):
    return lax.dot_general(left, right, (((1,), (1,)), ((), ())), preferred_element_type=F32)


def exchanged(value, mask):
    count = lax.axis_size("feat")
    return lax.ppermute(value, "feat", [(i, i ^ mask) for i in range(count)])


def ring(count):
    return [*range(0, count, 2), *range(count - 1, 0, -2)]


def passed_on(value, by):
    count = lax.axis_size("feat")
    order = ring(count)
    return lax.ppermute(value, "feat", [(order[p], order[(p + by) % count]) for p in range(count)])


def ring_owner(offset):
    count = COUNT
    me = lax.axis_index("feat")
    half = me // 2
    place = jnp.where(lax.rem(me, 2) == 0, half, count - 1 - half)
    place = lax.rem(place + offset + count, count)
    return jnp.where(place < count // 2, 2 * place, 2 * (count - 1 - place) + 1)


def split_kernel(in_ref, first_ref, last_ref, sems):
    middle = first_ref.shape[0]
    copies = [
        pltpu.make_async_copy(in_ref.at[:middle, :], first_ref, sems.at[0]),
        pltpu.make_async_copy(in_ref.at[middle:, :], last_ref, sems.at[1]),
    ]
    for copy in copies:
        copy.start()
    for copy in copies:
        copy.wait()


def ring_gather(own):
    count = lax.axis_size("feat")
    part = jax.ShapeDtypeStruct((own.shape[0] // 2, own.shape[1]), own.dtype)
    first, last = (
        {0: part}
        for part in pl.pallas_call(
            split_kernel,
            name="split",
            out_shape=(part, part),
            in_specs=[pl.BlockSpec(memory_space=pltpu.HBM)],
            out_specs=tuple(vmem(2)),
            scratch_shapes=[pltpu.SemaphoreType.DMA((2,))],
            compiler_params=params(2),
            cost_estimate=cost(SPLIT_FLOPS, 0),
        )(pltpu.with_memory_space_constraint(own, pltpu.HBM))
    )
    for step in range(1, count // 2):
        for held in (first, last):
            held[-step] = passed_on(held[1 - step], 1)
            held[step] = passed_on(held[step - 1], -1)
    far = count // 2
    first[far] = passed_on(first[1 - far], 1)
    last[far] = passed_on(last[far - 1], -1)
    return first, last


def owner(mask):
    return jnp.bitwise_xor(lax.axis_index("feat"), mask)


def columns(index, width):
    return pl.ds(pl.multiple_of(index * width, width), width)


def vmem(count):
    return [pl.BlockSpec(memory_space=pltpu.VMEM)] * count


def params(mib):
    return pltpu.CompilerParams(vmem_limit_bytes=mib * MIB)


def flat(groups):
    return [(i, row, mask) for i, masks in enumerate(groups) for row, mask in enumerate(masks)]


def pack_kernel(*refs):
    out_ref, start = refs[-1], 0
    for ref in refs[:-1]:
        out_ref[start : start + ref.shape[0], :] = ref[...]
        start += ref.shape[0]


def packed(*parts):
    rows = sum(part.shape[0] for part in parts)
    return pl.pallas_call(
        pack_kernel,
        name="pack",
        out_shape=jax.ShapeDtypeStruct((rows, parts[0].shape[1]), parts[0].dtype),
        in_specs=vmem(len(parts)),
        out_specs=vmem(1)[0],
        compiler_params=params(1),
        cost_estimate=pl.CostEstimate(
            flops=0, bytes_accessed=4 * rows * parts[0].shape[1], transcendentals=0
        ),
    )(*parts)


def block(parts, k):
    return jnp.concatenate([parts[2 * k][...], parts[2 * k + 1][...]], axis=0)


def pre_kernel(*refs):
    count = len(OFFSETS)
    parts, (w_ref, b_ref, codes_ref, active_ref) = refs[: 2 * count], refs[2 * count :]
    width = parts[0].shape[1]
    steps, tile = tiles(w_ref.shape[0])
    for j in range(steps):
        here = slice(j * tile, (j + 1) * tile)
        total = None
        for k, offset in enumerate(OFFSETS):
            term = against(w_ref[here, columns(ring_owner(offset), width)], block(parts, k))
            total = term if total is None else total + term
        active = jnp.maximum(total.T + b_ref[:, here], 0.0)
        active_ref[:, here] = active
        codes_ref[:, here] = (active * active).astype(BF16)


def decoded(w_ref, slot, here, parts, groups, tok, total):
    width = parts[0].shape[1]
    for i, row, mask in flat(groups):
        part = parts[i][row * tok : (row + 1) * tok, :]
        term = against(w_ref[slot, here, columns(owner(mask), width)], part)
        total = term if total is None else total + term
    return total


def tiles(size):
    tile = 256 if size % 256 == 0 else LANES
    return size // tile, tile


def own_recon_kernel(*refs):
    parts, (w_ref, total_ref) = refs[: len(BLOCKS)], refs[len(BLOCKS) :]
    tok = total_ref.shape[1]
    steps, tile = tiles(w_ref.shape[1])

    for j in range(steps):
        here = slice(j * tile, (j + 1) * tile)
        total_ref[here, :] = decoded(w_ref, 0, here, parts, BLOCKS, tok, None)


def near_recon_kernel(part_ref, before_ref, w_ref, total_ref):
    tok = total_ref.shape[1]
    steps, tile = tiles(w_ref.shape[1])
    for j in range(steps):
        here = slice(j * tile, (j + 1) * tile)
        total_ref[here, :] = decoded(w_ref, 1, here, [part_ref], BLOCKS[:1], tok, before_ref[here, :])


def products(error_ref, w_ref, slot, masks, out_ref):
    tok = error_ref.shape[0]
    for row, mask in enumerate(masks):
        term = jnp.dot(
            error_ref[...], w_ref[slot, :, columns(owner(mask), out_ref.shape[1])], preferred_element_type=F32
        )
        out_ref[row * tok : (row + 1) * tok, :] = term.astype(out_ref.dtype)


def recon_kernel(scale, *refs):
    rest = BLOCKS[1:]
    parts, (total_ref, w_ref, b_ref, target_ref, error_ref, far_ref) = refs[: len(rest)], refs[len(rest) :]
    tok = total_ref.shape[1]
    steps, tile = tiles(w_ref.shape[1])

    for j in range(steps):
        here = slice(j * tile, (j + 1) * tile)
        total = decoded(w_ref, 1, here, parts, rest, tok, total_ref[here, :])
        error = total.T + b_ref[:, here] - target_ref[:, here].astype(F32)
        error_ref[:, here] = (error * scale).astype(BF16)

    products(error_ref, w_ref, 1, FAR + CROSSING, far_ref)


def own_grad_kernel(error_ref, w_ref, sent_ref, near_ref, far_ref):
    products(error_ref, w_ref, 1, NEAR, sent_ref)
    products(error_ref, w_ref, 0, FAR + CROSSING, far_ref)
    products(error_ref, w_ref, 0, NEAR, near_ref)


def dec_grad_kernel(groups, *refs):
    error_ref, parts, out_ref = refs[0], refs[1 : 1 + len(groups)], refs[-1]
    width = parts[0].shape[1]
    tok = error_ref.shape[0]
    for i, row, mask in flat(groups):
        part = parts[i][row * tok : (row + 1) * tok, :]
        out_ref[0, 0, :, columns(owner(mask), width)] = transposed(error_ref[...], part).astype(BF16)


def add_kernel(count, first, own_ref, arrived_ref, *refs):
    for out_ref in refs[-count:]:
        here = slice(first, first + out_ref.shape[0])
        out_ref[...] = (own_ref[here, :] + arrived_ref[here, :].astype(F32)).astype(out_ref.dtype)
        first += out_ref.shape[0]


def enc_grad_kernel(*refs):
    grads, parts = refs[: -2 - 2 * COUNT], refs[-2 - 2 * COUNT : -2]
    active_ref, out_ref = refs[-2:]
    width = parts[0].shape[1]
    total = grads[0][...]
    for grad in grads[1:]:
        total = total + grad[...].astype(F32)
    pre_grad = (total * 2.0 * active_ref[...]).astype(BF16)
    for k, offset in enumerate(OFFSETS):
        out_ref[0, :, columns(ring_owner(offset), width)] = transposed(pre_grad, block(parts, k)).astype(BF16)


def cost(flops, moved):
    return pl.CostEstimate(flops=flops, bytes_accessed=moved, transcendentals=0)


def on_device(inputs, targets, enc_w, enc_b, dec_w, dec_b):
    count = COUNT
    tok, width = inputs.shape[1:]
    own_features, model = enc_w.shape[1:]
    features = dec_w.shape[3]
    scale = tok ** (-0.5)
    matmul = 2 * tok * width * features
    struct = jax.ShapeDtypeStruct

    def stack(masks, kind):
        return struct((len(masks) * tok, own_features), kind)


    first, last = ring_gather(inputs[0])
    inputs_of = [part for offset in OFFSETS for part in (first[offset], last[offset])]
    enc_weights, weights = [pltpu.with_memory_space_constraint(w[0], pltpu.VMEM) for w in (enc_w, dec_w)]

    codes, active = pl.pallas_call(
        pre_kernel,
        name="pre",
        out_shape=(struct((tok, own_features), BF16), struct((tok, own_features), F32)),
        in_specs=vmem(2 * count + 2),
        out_specs=tuple(vmem(2)),
        compiler_params=params(16),
        cost_estimate=cost(2 * tok * own_features * model, 0),
    )(*inputs_of, enc_weights, enc_b)

    far_pair = packed(exchanged(codes, 6), exchanged(codes, 4))
    far_across = exchanged(far_pair, 1)
    own = [packed(codes, *[exchanged(codes, mask) for mask in (1, 2, 3)]), far_pair, far_across]
    previous = [from_behind(part, "section", 1) for part in own]

    total = pl.pallas_call(
        own_recon_kernel,
        name="own_recon",
        out_shape=struct((width, tok), F32),
        in_specs=vmem(len(own) + 1),
        out_specs=vmem(1)[0],
        compiler_params=params(8),
        cost_estimate=cost(matmul, 0),
    )(*own, weights)

    total = pl.pallas_call(
        near_recon_kernel,
        name="near_recon",
        out_shape=struct((width, tok), F32),
        in_specs=vmem(3),
        out_specs=vmem(1)[0],
        compiler_params=params(8),
        cost_estimate=cost(matmul // 2, 0),
    )(previous[0], total, weights)

    error, sent_far = pl.pallas_call(
        functools.partial(recon_kernel, scale),
        name="recon",
        out_shape=(struct((tok, width), BF16), stack(FAR + CROSSING, BF16)),
        in_specs=vmem(len(previous) + 3),
        out_specs=tuple(vmem(2)),
        compiler_params=params(8),
        cost_estimate=cost(2 * matmul, 4 * MIB),
    )(*previous[1:], total, weights, dec_b, targets[0])
    arrived_far = from_behind(sent_far, "section", -1)

    sent_near, own_near, own_far = pl.pallas_call(
        own_grad_kernel,
        name="own_grad",
        out_shape=(stack(NEAR, BF16), stack(NEAR, F32), stack(FAR + CROSSING, F32)),
        in_specs=vmem(2),
        out_specs=tuple(vmem(3)),
        compiler_params=params(8),
        cost_estimate=cost(3 * matmul // 2, 6 * MIB),
    )(error, weights)
    arrived_near = from_behind(sent_near, "section", -1)

    rows = 256 if width % 256 == 0 else LANES

    def sums(outs, own_part, arrived, *after, first=0):
        return pl.pallas_call(
            functools.partial(add_kernel, len(outs), first),
            name="sum",
            out_shape=tuple(stack(masks, kind) for masks, kind in outs),
            in_specs=[*vmem(2), *[pl.BlockSpec(memory_space=kind) for _, kind in after]],
            out_specs=tuple(vmem(len(outs))),
            compiler_params=params(2),
            cost_estimate=cost(tok * features, 2 * MIB),
        )(own_part, arrived, *[value for value, _ in after])

    def dec_grad_slot(slot, groups, parts, before, held):
        return pl.pallas_call(
            functools.partial(dec_grad_kernel, groups),
            name="dec_grad",
            grid=(width // rows,),
            out_shape=struct(dec_w.shape, BF16),
            in_specs=[
                pl.BlockSpec((tok, rows), lambda j: (0, j)),
                *[pl.BlockSpec(part.shape, lambda j: (0, 0)) for part in parts],
                pl.BlockSpec(memory_space=pltpu.HBM) if held else pl.BlockSpec(memory_space=pl.ANY),
            ],
            out_specs=pl.BlockSpec((1, 1, rows, features), lambda j: (0, slot, j, 0)),
            input_output_aliases={1 + len(parts): 0} if held else {},
            compiler_params=params(12),
            cost_estimate=cost(matmul, 2 * width * features),
        )(error, *parts, before)

    kept, crossing = sums(((FAR, F32), (CROSSING, BF16)), own_far, arrived_far)
    dec_grad = dec_grad_slot(0, BLOCKS, own, crossing, False)
    held_grad = pltpu.with_memory_space_constraint(dec_grad, pltpu.HBM)
    lines = sums(
        [((mask,), BF16) for mask in FAR], kept, exchanged(crossing, 1), (held_grad, pltpu.HBM)
    )
    mine, across = sums([((0,), F32), ((1,), BF16)], own_near, arrived_near, (lines[0], pltpu.VMEM))
    across = exchanged(across, 1)
    near = sums(
        [((2,), BF16), ((3,), BF16)], own_near, arrived_near, (across, pltpu.VMEM), first=2 * tok
    )
    grads = [
        mine,
        across,
        *[exchanged(line, mask) for mask, line in zip(FAR, lines)],
        *[exchanged(part, mask) for mask, part in zip((2, 3), near)],
    ]
    dec_grad = dec_grad_slot(1, BLOCKS, previous, held_grad, True)

    block_rows = tiles(own_features)[1]
    enc_grad = pl.pallas_call(
        enc_grad_kernel,
        name="enc_grad",
        grid=(own_features // block_rows,),
        out_shape=struct(enc_w.shape, BF16),
        in_specs=[
            *[pl.BlockSpec((tok, block_rows), lambda j: (0, j))] * len(grads),
            *[pl.BlockSpec((tok // 2, width), lambda j: (0, 0))] * (2 * count),
            pl.BlockSpec((tok, block_rows), lambda j: (0, j)),
        ],
        out_specs=pl.BlockSpec((1, block_rows, model), lambda j: (0, j, 0)),
        compiler_params=params(24),
        cost_estimate=cost(matmul, 2 * own_features * model),
    )(*grads, *inputs_of, active)
    return enc_grad, dec_grad


def plain(inputs, targets, enc_w, enc_b, dec_w, dec_b):
    scale = inputs.shape[1] ** (-0.5)
    gathered = lax.all_gather(inputs[0], "feat", axis=1, tiled=True)
    active = jnp.maximum(against(gathered, enc_w[0]) + enc_b[0], 0.0)
    codes = (active * active).astype(BF16)
    own = lax.all_gather(codes, "feat", axis=1, tiled=True)
    previous = from_behind(own, "section", 1)
    weights = dec_w[0]
    total = dec_b[0] + against(own, weights[0]) + against(previous, weights[1])
    error = ((total - targets[0].astype(F32)) * scale).astype(BF16)
    sent = jnp.dot(error, weights[1], preferred_element_type=F32)
    code_grad = jnp.dot(error, weights[0], preferred_element_type=F32) + from_behind(sent, "section", -1)
    mine = lax.psum_scatter(code_grad, "feat", scatter_dimension=1, tiled=True)
    pre_grad = (mine * 2.0 * active).astype(BF16)
    enc_grad = transposed(pre_grad, gathered).astype(BF16)[None]
    dec_grad = jnp.stack([transposed(error, source).astype(BF16) for source in (own, previous)])[None]
    return enc_grad, dec_grad


def chosen(inputs, targets, enc_w, enc_b, dec_w, dec_b):
    aligned = all(size % LANES == 0 for size in (*inputs.shape[1:], enc_w.shape[1]))
    fits = lax.axis_size("feat") == COUNT and dec_w.shape[1] == 2
    body = on_device if aligned and fits else plain
    return body(inputs, targets, enc_w, enc_b, dec_w, dec_b)


def solution(mesh):
    return jax.shard_map(
        chosen,
        mesh=mesh,
        in_specs=(
            P("section", None, "feat"),
            P("section", None, "feat"),
            P("section", "feat", None),
            P("section", "feat"),
            P("section", None, "feat", None),
            P("section", "feat"),
        ),
        out_specs=(P("section", "feat", None), P("section", None, "feat", None)),
        check_vma=False,
    )
```
